512 devices in a mesh: dp: 8 (over z), expert: 64 (over x, y, core).
Axes of the slice: x: 4, y: 8, z: 8, core: 2. Of those that a mesh axis runs over, the one named last changes fastest.
Arguments:
- query_nope: bfloat16 [2048, 128, 128], P(('dp', 'expert')), may hold values from -6 to 6
- query_rope: bfloat16 [2048, 128, 64], P(('dp', 'expert')), may hold values from -320 to 320
- latent_cache: bfloat16 [2048, 512, 512], P(('dp', 'expert')), may hold values from -6 to 6
- key_rope: bfloat16 [2048, 512, 64], P(('dp', 'expert')), may hold values from -4 to 4
- lengths: int32 [2048], P(('dp', 'expert')), may hold values from 64 to 512, as said below
- key_weight: bfloat16 [128, 128, 512], P('expert', 'dp'), may hold values from -0.5 to 0.5
- expert_input: bfloat16 [2048, 7168], P(('dp', 'expert')), may hold values from -6 to 6
- route_slots: int32 [2048, 2], P(('dp', 'expert')), may hold values from 0 to 7, all different within a row; in each aligned block of 4 rows (0 to 3, 4 to 7, ...) at most 2 rows name the same one
- route_gates: float32 [2048, 2], P(('dp', 'expert')), may hold values from 0.1 to 1
- trainer_gate_up: bfloat16 [8, 2048, 2, 7168], P(None, 'expert', None, 'dp'), may hold values from -0.0625 to 0.0625
- trainer_down: bfloat16 [8, 2048, 7168], P(None, 'expert', 'dp'), may hold values from -0.125 to 0.125
- trainer_order: int32 [8], replicated, may hold values from 0 to 7, each once
- rollout_order: int32 [8], replicated, may hold values from 0 to 7, each once
Outputs:
- latent_output: bfloat16 [2048, 128, 512], P(('dp', 'expert'))
- expert_output: bfloat16 [2048, 7168], P(('dp', 'expert'))
The draws below stay inside these ranges and needn't reach their ends.
Inputs may be any that keep to these rules, and one draw needn't show every extreme that they name: `route_slots`: each row names 2 different slots. Within the rows of one device (aligned blocks of 4 rows) no slot is named by more than 2 rows, and in some block a slot is named by exactly 2 rows. A permutation: trainer position i holds expert trainer_order[i]. A permutation: rollout slot g holds expert rollout_order[g]. `lengths`: among the rows of one device some row has exactly 512 positions.
All inputs are finite; a program needn't handle non-finite values.
Results may differ from the reference program's by a relative error of at most 0.0069.
Values may be sent and summed in bfloat16 or wider, within the bound.
A program may use at most 128 MiB of HBM per device.

```python
import math
import jax
import jax.numpy as jnp
import numpy as np
from jax import lax

D = 7168
HEADS = 128
NOPE = 128
ROPE = 64
RANK = 512
FF = 2048
SLAB = 8
TOPK = 2
ROW_DEV = 4
CACHE = 512
CAP = 2
GROUP = 8
ROWS = 2048
N_EXPERT = 64


def rope_common(key):
    base = jax.random.normal(jax.random.fold_in(key, 101), (ROWS, CACHE, ROPE), jnp.float32)
    base = jnp.clip(base, -4.0, 4.0)
    return base


def draw_key_rope(key, part):
    base = rope_common(key)
    return base.astype(jnp.bfloat16)


def draw_query_rope(key, part):
    key = jax.random.fold_in(key, 9)
    streams = jax.random.split(key, 1)
    values = jnp.clip(jax.random.normal(streams[0], (ROWS, HEADS, ROPE), jnp.float32), -4.0, 4.0)
    return values.astype(jnp.bfloat16)


def draw_lengths(key, part):
    key = jax.random.fold_in(key, 5)
    streams = jax.random.split(key, 2)
    drawn = jax.random.randint(streams[0], (ROWS,), CACHE // 8, CACHE + 1)
    full_row = jax.random.randint(streams[1], (ROWS // ROW_DEV,), 0, ROW_DEV)
    places = jnp.arange(ROWS)
    marked = places % ROW_DEV == jnp.repeat(full_row, ROW_DEV, total_repeat_length=ROWS)
    return jnp.where(marked, CACHE, drawn).astype(jnp.int32)


def shard_levels(rng, extent, cuts, least, high):
    level, own = 1.0, jax.random.fold_in(rng, 6)
    for dim, shards_of in cuts:
        draws = jnp.exp(jax.random.uniform(jax.random.fold_in(own, dim), (shards_of,), jnp.float32, least / len(cuts), high / len(cuts)))
        level = level * jnp.repeat(draws, extent[dim] // shards_of).reshape([-1 if axis == dim else 1 for axis in range(len(extent))])
    return level


def routed_block(own_key, own, number, rows, amount, top, most, slope):
    ranking = jax.random.permutation(own_key, amount)
    heavy_load, common = load_shares(amount, rows * top, most, slope, True), load_shares(amount, rows * top, most, slope, False)
    places = jnp.arange(amount)

    def named(sizes, rotation):
        used = int((sizes > 0).sum())
        fixed = max(1, used // 4)
        moved = fixed + (places - fixed + rotation * (used - fixed)) % max(1, amount - fixed)
        return jnp.zeros((amount,), jnp.int32).at[ranking[jnp.where(places < fixed, places, moved)]].set(jnp.asarray(sizes, jnp.int32))

    sizes = jnp.where(number % 4 == 0, named(heavy_load, number // 4), named(common, number - number // 4 - 1))
    mixed = jax.random.permutation(jax.random.fold_in(own, 3), amount)
    source_of, receiver = mixed[0:amount // 2 * 2:2], mixed[1:amount // 2 * 2:2]
    slack = jnp.minimum(sizes[source_of] - 1, most - sizes[receiver]) // 2
    slack = jnp.where((source_of == ranking[0]) | (receiver == ranking[0]) | (sizes[receiver] == 0), 0, jnp.maximum(slack, 0))
    moved = jax.random.randint(jax.random.fold_in(own, 4), (amount // 2,), 0, 1 << 20) % (slack + 1)
    sizes = sizes.at[source_of].add(-moved).at[receiver].add(moved)
    members = jnp.searchsorted(jnp.cumsum(sizes), jnp.arange(rows * top), side="right").astype(jnp.int32)
    grid = members.reshape(top, rows).T
    grid = grid[jax.random.permutation(jax.random.fold_in(own, 1), rows)]
    rotation = jax.random.randint(jax.random.fold_in(own, 2), (rows, 1), 0, top)
    return jnp.take_along_axis(grid, (jnp.arange(top)[None, :] + rotation) % top, axis=1)


def load_shares(number_of, total, bound, slope, full):
    portions = [(1 << 20) // math.isqrt(standing ** slope) + 1 for standing in range(1, number_of + 1)]
    largest = bound if full else min(bound, max(-(-total // number_of), total * portions[0] // sum(portions)))
    least = 1 if total - largest >= number_of - 1 else 0
    holding, spare = [largest] + [least] * (number_of - 1), total - largest - least * (number_of - 1)
    while spare > 0:
        movable = [i for i in range(1, number_of) if holding[i] < largest] or [i for i in range(1, number_of) if holding[i] < bound]
        pool, budget = sum([portions[i] for i in movable]), spare
        for i in movable:
            extra = min(bound - holding[i], max(1, budget * portions[i] // pool), spare)
            holding[i] = holding[i] + extra
            spare = spare - extra
    return np.array(holding)


def normal_values(stream_key, extent, scale, bound, cuts=(), kind=jnp.bfloat16):
    values = scale * jax.random.normal(stream_key, extent, jnp.float32)
    if cuts:
        values = values * shard_levels(stream_key, extent, cuts, -0.22, 0.18)
    return jnp.clip(values, -bound, bound).astype(kind)


def setup_inputs(seed: int = 0) -> dict:
    key_list = jax.random.split(jax.random.key(seed), 14)
    query_nope = normal_values(key_list[0], (ROWS, HEADS, NOPE), 1.0, 6.0, ((0, 512),))
    query_rope = draw_query_rope(jax.random.fold_in(key_list[13], 71), 0)
    latent_cache = normal_values(key_list[2], (ROWS, CACHE, RANK), 1.0, 6.0, ((0, 512),))
    key_rope = draw_key_rope(jax.random.fold_in(key_list[13], 71), 0)
    lengths = draw_lengths(jax.random.fold_in(key_list[13], 71), 0)
    key_weight = normal_values(key_list[5], (HEADS, NOPE, RANK), NOPE ** -0.5, 0.5, ((0, 64), (1, 8)))
    expert_input = normal_values(key_list[6], (ROWS, D), 1.0, 6.0, ((0, 512),))
    route_slots_keys = jax.random.split(jax.random.fold_in(key_list[7], 1), ROWS // ROW_DEV)
    route_slots_turns = jax.random.permutation(jax.random.fold_in(key_list[7], 3), ROWS // ROW_DEV)
    route_slots = jax.vmap(lambda own, number: routed_block(jax.random.fold_in(key_list[7], 2), own, number, ROW_DEV, SLAB, TOPK, CAP, 2))(route_slots_keys, route_slots_turns).reshape((ROWS, TOPK))
    route_gates = jnp.clip(jnp.exp(math.log(1.0) - 2.3025851 * jax.random.uniform(key_list[8], (ROWS, TOPK), jnp.float32) ** shard_levels(key_list[8], (ROWS, TOPK), ((0, 512),), -0.2, 0.2)), 0.1, 1.0)
    trainer_gate_up = normal_values(key_list[9], (SLAB, FF, 2, D), D ** -0.5, 0.0625, ((1, 64), (3, 8)))
    trainer_down = normal_values(key_list[10], (SLAB, FF, D), FF ** -0.5, 0.125, ((1, 64), (2, 8)))
    trainer_order = jax.random.permutation(key_list[11], SLAB).astype(jnp.int32)
    rollout_order = jax.random.permutation(key_list[12], SLAB).astype(jnp.int32)
    return dict(query_nope=query_nope, query_rope=query_rope, latent_cache=latent_cache, key_rope=key_rope, lengths=lengths, key_weight=key_weight, expert_input=expert_input, route_slots=route_slots, route_gates=route_gates, trainer_gate_up=trainer_gate_up, trainer_down=trainer_down, trainer_order=trainer_order, rollout_order=rollout_order)


def reference(query_nope, query_rope, latent_cache, key_rope, lengths, key_weight, expert_input, route_slots, route_gates, trainer_gate_up, trainer_down, trainer_order, rollout_order):
    block_rows = ROW_DEV * N_EXPERT
    blocks = ROWS // block_rows
    score_scale = 1.0 / math.sqrt(NOPE + ROPE)
    weight_wide = key_weight.astype(jnp.float32)

    def attend(pieces):
        nope_part, rope_part, cache_part, key_part, length_part = pieces
        query_latent = jnp.einsum('rhn,hnk->rhk', nope_part.astype(jnp.float32), weight_wide).astype(jnp.bfloat16)
        cache_wide = cache_part.astype(jnp.float32)
        scores = jnp.einsum('rhk,rlk->rhl', query_latent.astype(jnp.float32), cache_wide)
        scores = scores + jnp.einsum('rhp,rlp->rhl', rope_part.astype(jnp.float32), key_part.astype(jnp.float32))
        scores = scores * score_scale
        visible = jnp.arange(CACHE, dtype=jnp.int32)[None, None, :] < length_part[:, None, None]
        scores = jnp.where(visible, scores, -jnp.inf)
        highest = lax.optimization_barrier(jnp.max(scores, axis=2, keepdims=True))
        raised = jnp.exp(scores - highest)
        attention = (raised / lax.optimization_barrier(jnp.sum(raised, axis=2, keepdims=True))).astype(jnp.bfloat16)
        return jnp.einsum('rhl,rlk->rhk', attention.astype(jnp.float32), cache_wide).astype(jnp.bfloat16)
    pieces = (query_nope.reshape(blocks, block_rows, HEADS, NOPE), query_rope.reshape(blocks, block_rows, HEADS, ROPE), latent_cache.reshape(blocks, block_rows, CACHE, RANK), key_rope.reshape(blocks, block_rows, CACHE, ROPE), lengths.reshape(blocks, block_rows))
    latent_output = lax.map(attend, pieces).reshape(ROWS, HEADS, RANK)
    positions = jnp.arange(SLAB, dtype=jnp.int32)

    def slot_step(running, slot_index):
        position = jnp.sum(jnp.where(trainer_order == rollout_order[slot_index], positions, 0)).astype(jnp.int32)
        gate_up = lax.dynamic_index_in_dim(trainer_gate_up, position, 0, keepdims=False)
        down_rows = lax.dynamic_index_in_dim(trainer_down, position, 0, keepdims=False)
        gate_value = jnp.dot(expert_input, gate_up[:, 0, :].T, preferred_element_type=jnp.float32)
        up_value = jnp.dot(expert_input, gate_up[:, 1, :].T, preferred_element_type=jnp.float32)
        hidden = (jax.nn.silu(gate_value) * up_value).astype(jnp.bfloat16)
        hidden_classes = hidden.reshape(ROWS, FF // GROUP, GROUP)
        down_classes = down_rows.reshape(FF // GROUP, GROUP, D)
        summed = jnp.zeros((ROWS, D), jnp.float32)
        for member in range(GROUP):
            class_share = jnp.dot(hidden_classes[:, :, member], down_classes[:, member, :], preferred_element_type=jnp.float32).astype(jnp.bfloat16)
            summed = summed + class_share.astype(jnp.float32)
        factor = lax.optimization_barrier(jnp.sum(jnp.where(route_slots == slot_index, route_gates, jnp.zeros_like(route_gates)), axis=1))
        return (running + factor[:, None] * summed, None)
    running, unused = lax.scan(slot_step, jnp.zeros((ROWS, D), jnp.float32), positions)
    expert_output = running.astype(jnp.bfloat16)
    return (latent_output, expert_output)
```

```python
import math

import jax
import jax.numpy as jnp
import numpy as np
from jax import lax
from jax.experimental import pallas as pl
from jax.experimental.pallas import tpu as pltpu
from jax.sharding import PartitionSpec as P

NOPE = 128
ROPE = 64
NX, NY, NZ = 4, 8, 8
BF = jnp.bfloat16
F32 = jnp.float32
MESH = pl.DeviceIdType.MESH
X_ORDER = (0, 1, 3, 2)
FORWARD_PLUS = (0, 2, 5, 7)
FORWARD_MINUS = (1, 3, 4, 6)


def constants():
    perm = np.zeros((256, 256), np.float32)
    for z in range(8):
        for t in range(8):
            for r in range(4):
                perm[t * 32 + z * 4 + r, z * 32 + t * 4 + r] = 1
    col = np.arange(512)
    mask_in = np.zeros((128, 1024), np.float32)
    pick = np.zeros((1024, 128), np.float32)
    for k in range(2):
        mask_in[k * 8 + col // 64, k * 512 + col] = 1
        pick[k * 512 + col, (col % 2) * 64 + k * 32 + (col % 64) // 2] = 1
    gate = np.zeros((128, 128), np.float32)
    for k in range(2):
        for j in range(3):
            gate[16 + 3 * k + j, k * 32 : k * 32 + 32] = 1
    spread = np.zeros((2, 128, 512), np.float32)
    mask_out = np.zeros((128, 512), np.float32)
    unit = np.arange(256)
    for k in range(2):
        mask_out[k * 8 + unit // 32, k * 256 + unit] = 1
        for c in range(2):
            spread[c, c * 64 + k * 32 + unit % 32, k * 256 + unit] = 1
    repeat = np.zeros((128, 512), np.float32)
    repeat[((col // 32) % 8) * 16 + col % 16, col] = 1
    return [
        jnp.asarray(a, BF) for a in (perm, perm.T, mask_in, pick, gate, spread, mask_out, repeat)
    ]


def dot(a, b):
    return jnp.dot(a, b, preferred_element_type=F32)


def dot_nt(a, b):
    return lax.dot_general(a, b, (((1,), (1,)), ((), ())), preferred_element_type=F32)


def kernel(
    pieces, w_in, w_out, key_own, q_send,
    perm, perm_t, mask_in, pick, gate, spread, mask_out, repeat,
    out_rows, out_latent,
    got, rows, part, part_got, hid, share, share_sib, ring_out, ring_in, col_sum, col_got,
    back_out, back_got, keys, q_col, q_own, lat_own, lat_col, lat_got,
    s_piece, r_piece, s_ring, r_ring, s_x, r_x, s_fwd, r_fwd, s_sib, r_sib,
    s_part, r_part, s_hid, r_hid, s_ssib, r_ssib, s_red, r_red, s_col, r_col, s_back, r_back,
    s_key, r_key, s_ksib, r_ksib, s_qy, r_qy, s_qx, r_qx, s_ly, r_ly, s_lx, r_lx,
):
    z = lax.axis_index("dp")
    e = lax.axis_index("expert")
    c = lax.rem(e, 2)
    y = lax.rem(e // 2, NY)
    x = e // (2 * NY)
    sign = 1 - 2 * c

    def at_z(d):
        return lax.rem(z + d, NZ)

    def at_x(d):
        return lax.rem(x + d, NX)

    def at_y(d):
        return lax.rem(y + NY + d, NY)

    def on_z(d):
        return (at_z(d), e)

    def on_x(d):
        return (z, (at_x(d) * NY + y) * 2 + c)

    def on_y(d):
        return (z, (x * NY + at_y(d)) * 2 + c)

    sibling = (z, e + 1 - 2 * c)

    barrier = pltpu.get_barrier_semaphore()
    peers = [on_z(d) for d in range(1, NZ)] + [on_y(d) for d in range(1, NY)]
    peers += [on_x(d) for d in range(1, NX)] + [sibling]
    for peer in peers:
        pl.semaphore_signal(barrier, inc=1, device_id=peer, device_id_type=MESH)
    pl.semaphore_wait(barrier, len(peers))

    sent = []

    def send(src, dst, s_sem, r_sem, peer):
        copy = pltpu.make_async_remote_copy(
            src_ref=src, dst_ref=dst, send_sem=s_sem, recv_sem=r_sem,
            device_id=peer, device_id_type=MESH,
        )
        copy.start()
        sent.append(copy)
        return copy

    piece = [
        send(pieces.at[at_z(d)], got.at[z], s_piece.at[d - 1], r_piece.at[d - 1], on_z(d))
        for d in range(1, NZ)
    ]
    key_z = [
        send(key_own, keys.at[c, z], s_key.at[d - 1], r_key.at[d - 1], on_z(d))
        for d in range(1, NZ)
    ]
    q_y = [
        send(q_send.at[at_y(d)], q_col.at[y], s_qy.at[d - 1], r_qy.at[d - 1], on_y(d))
        for d in range(1, NY)
    ]
    got[z] = pieces[z]
    keys[c, z] = key_own[...]
    q_col[y] = q_send[y]

    for copy in piece:
        copy.wait_recv()
    turned = dot(perm[...], got[...].reshape(256, 128)).astype(BF)
    for t in range(8):
        rows[x, c, y, :, t * 128 : (t + 1) * 128] = turned[t * 32 : (t + 1) * 32]

    def block(xi, yi):
        return rows.at[xi, c, yi]

    origins, x_plus, x_minus = [], [], []

    def to_x(origin):
        k = len(origins)
        origins.append(origin)
        b = block(x, origin)
        x_plus.append(send(b, b, s_x.at[0, k], r_x.at[0, k], on_x(1)))
        x_minus.append(send(b, b, s_x.at[1, k], r_x.at[1, k], on_x(3)))

    def ring(origin, way, step):
        b = block(x, origin)
        peer = on_y(sign) if way == 0 else on_y(-sign)
        return send(b, b, s_ring.at[way, step], r_ring.at[way, step], peer)

    plus, minus = ring(y, 0, 0), ring(y, 1, 0)
    to_x(y)
    q_x = None
    for step in range(1, 5):
        plus.wait_recv()
        origin = at_y(-sign * step)
        if step < 4:
            plus = ring(origin, 0, step)
        to_x(origin)
        if step < 4:
            minus.wait_recv()
            origin = at_y(sign * step)
            if step < 3:
                minus = ring(origin, 1, step)
            to_x(origin)
        if step == 1:
            for copy in q_y:
                copy.wait_recv()
            q_x = [
                send(q_col.at[:, at_x(d)], q_own.at[x], s_qx.at[d - 1], r_qx.at[d - 1], on_x(d))
                for d in range(1, NX)
            ]
            q_own[x] = q_col[:, x]
        if step == 2:
            for copy in key_z:
                copy.wait_recv()
            key_sib = send(keys.at[c], keys.at[c], s_ksib.at[0], r_ksib.at[0], sibling)

    def to_sibling(j):
        b = rows.at[at_x(X_ORDER[j]), c]
        return send(b, b, s_sib.at[j], r_sib.at[j], sibling)

    def project(j):
        xi = at_x(X_ORDER[j])

        def body(ci, carry):
            routing = rows[xi, ci, :, :, 896:1024].reshape(256, 128)
            mask = dot(routing, mask_in[...])
            values = dot_nt(rows[xi, ci, :, :, 0:896].reshape(256, 896), w_in[...])
            first = (values * mask[:, :512]).astype(BF)
            second = (values * mask[:, 512:]).astype(BF)
            picked = dot(first, pick[0:512, :]) + dot(second, pick[512:1024, :])
            part[j, :, pl.ds(pl.multiple_of(ci * 32, 32), 32), :] = picked.astype(BF).reshape(
                8, 32, 128
            )
            return carry

        lax.fori_loop(0, 2, body, 0)
        return [
            send(
                part.at[j, at_z(d)], part_got.at[j, d - 1],
                s_part.at[j, d - 1], r_part.at[j, d - 1], on_z(d),
            )
            for d in range(1, NZ)
        ]

    def activate(j, arriving):
        xi = at_x(X_ORDER[j])
        for copy in arriving:
            copy.wait_recv()
        total = part[j, z].astype(F32)
        for d in range(7):
            total = total + part_got[j, d].astype(F32)
        up = pltpu.roll(total, 64, 1)
        routing = rows[xi, :, z, :, 896:1024].reshape(64, 128)
        value = total / (1.0 + jnp.exp(-total)) * up * dot(routing, gate[...])
        lane = lax.broadcasted_iota(jnp.int32, (32, 128), 1)
        packed = jnp.where(lane < 64, value[0:32], pltpu.roll(value[32:64], 64, 1))
        hid[j, z] = packed.astype(BF)
        return [
            send(
                hid.at[j, z], hid.at[j, z],
                s_hid.at[j, d - 1], r_hid.at[j, d - 1], on_z(d),
            )
            for d in range(1, NZ)
        ]

    def project_down(j, arriving):
        xi = at_x(X_ORDER[j])
        for copy in arriving:
            copy.wait_recv()

        def body(ci, carry):
            routing = rows[xi, ci, :, :, 896:1024].reshape(256, 128)
            wide = dot(hid[j].reshape(256, 128), spread[ci]) * dot(routing, mask_out[...])
            dense = (wide[:, :256] + wide[:, 256:]).astype(BF)
            share[j, ci] = dot(dense, w_out[...]).astype(BF).reshape(8, 32, 896)
            return carry

        lax.fori_loop(0, 2, body, 0)
        return send(
            share.at[j, 1 - c], share_sib.at[j], s_ssib.at[j], r_ssib.at[j], sibling
        )

    def own_share(j, target):
        return share[j, c, target].astype(F32) + share_sib[j, target].astype(F32)

    def reduce_step(j, step, state):
        new = [None, None]
        if step == 1:
            state.wait_recv()
        for way, hops in ((0, 4), (1, 3)):
            if step > hops:
                new[way] = state[way]
                continue
            target = at_y(sign * (hops + 1 - step) * (1 - 2 * way))
            value = own_share(j, target)
            if step > 1:
                state[way].wait_recv()
                value = value + ring_in[j, way, step - 2].astype(F32)
            ring_out[j, way, step - 1] = value.astype(BF)
            new[way] = send(
                ring_out.at[j, way, step - 1], ring_in.at[j, way, step - 1],
                s_red.at[j, way, step - 1], r_red.at[j, way, step - 1],
                on_y(sign * (1 - 2 * way)),
            )
        return new

    def reduce_end(j, state):
        state[0].wait_recv()
        state[1].wait_recv()
        value = own_share(j, y) + ring_in[j, 0, 3].astype(F32) + ring_in[j, 1, 2].astype(F32)
        col_sum[j] = value.astype(BF)
        if j == 0:
            return None
        return send(
            col_sum.at[j], col_got.at[j - 1], s_col.at[j - 1], r_col.at[j - 1], on_x(X_ORDER[j])
        )

    def absorb():
        for copy in q_x:
            copy.wait_recv()
        key_sib.wait_recv()
        wide = dot(q_own[...].reshape(512, 128), repeat[...])
        row = lax.broadcasted_iota(jnp.int32, (512, 512), 0)
        lane = lax.broadcasted_iota(jnp.int32, (512, 512), 1)
        head = (lane // 256) * 2 + (lane // 16) % 2
        wide = jnp.where(row % 4 == head, wide, 0.0).astype(BF)
        lat_own[...] = dot(wide, keys[...].reshape(512, 512)).astype(BF).reshape(4, 8, 16, 512)
        copies = [
            send(lat_own.at[:, at_y(d)], lat_col.at[y], s_ly.at[d - 1], r_ly.at[d - 1], on_y(d))
            for d in range(1, NY)
        ]
        lat_col[y] = lat_own[:, y]
        return copies

    def latent_x(arriving):
        for copy in arriving:
            copy.wait_recv()
        copies = [
            send(lat_col.at[:, at_x(d)], lat_got.at[x], s_lx.at[d - 1], r_lx.at[d - 1], on_x(d))
            for d in range(1, NX)
        ]
        lat_got[x] = lat_col[:, x]
        return copies

    sib = [to_sibling(0)]
    lat_y = absorb()
    sib[0].wait_recv()
    parts = [project(0)]
    far = []
    for k in range(8):
        x_minus[k].wait_recv()
        if k in FORWARD_MINUS:
            b = block(at_x(1), origins[k])
            far.append(send(b, b, s_fwd.at[k], r_fwd.at[k], on_x(3)))
        x_plus[k].wait_recv()
        if k in FORWARD_PLUS:
            b = block(at_x(3), origins[k])
            far.append(send(b, b, s_fwd.at[k], r_fwd.at[k], on_x(1)))
    sib.append(to_sibling(1))
    sib.append(to_sibling(2))
    hids = [activate(0, parts[0])]
    sib[1].wait_recv()
    parts.append(project(1))
    downs = [project_down(0, hids[0])]
    sib[2].wait_recv()
    parts.append(project(2))
    hids.append(activate(1, parts[1]))
    red = [reduce_step(0, 1, downs[0])]
    downs.append(project_down(1, hids[1]))
    hids.append(activate(2, parts[2]))
    red[0] = reduce_step(0, 2, red[0])
    red.append(reduce_step(1, 1, downs[1]))
    for copy in far:
        copy.wait_recv()
    sib.append(to_sibling(3))
    lat_x = latent_x(lat_y)
    downs.append(project_down(2, hids[2]))
    red[0] = reduce_step(0, 3, red[0])
    sib[3].wait_recv()
    parts.append(project(3))
    red[1] = reduce_step(1, 2, red[1])
    red.append(reduce_step(2, 1, downs[2]))
    red[0] = reduce_step(0, 4, red[0])
    hids.append(activate(3, parts[3]))
    red[1] = reduce_step(1, 3, red[1])
    red[2] = reduce_step(2, 2, red[2])
    downs.append(project_down(3, hids[3]))
    red.append(reduce_step(3, 1, downs[3]))
    red[1] = reduce_step(1, 4, red[1])
    red[2] = reduce_step(2, 3, red[2])
    red[3] = reduce_step(3, 2, red[3])
    reduce_end(0, red[0])
    cols = [reduce_end(1, red[1])]
    red[2] = reduce_step(2, 4, red[2])
    red[3] = reduce_step(3, 3, red[3])
    cols.append(reduce_end(2, red[2]))
    red[3] = reduce_step(3, 4, red[3])
    for copy in lat_x:
        copy.wait_recv()
    out_latent[...] = lat_got[...]
    cols.append(reduce_end(3, red[3]))

    total = col_sum[0].astype(F32)
    for j in range(3):
        cols[j].wait_recv()
        total = total + col_got[j].astype(F32)
    total = total.astype(BF)
    tiles = [total[:, t * 128 : (t + 1) * 128] for t in range(7)] + [jnp.zeros((32, 128), BF)]
    tiles = jnp.concatenate(tiles, axis=0)
    back_out[...] = dot(perm_t[...], tiles).astype(BF).reshape(8, 32, 128)
    back = [
        send(back_out.at[at_z(d)], back_got.at[z], s_back.at[d - 1], r_back.at[d - 1], on_z(d))
        for d in range(1, NZ)
    ]
    back_got[z] = back_out[z]
    for copy in back:
        copy.wait_recv()
    out_rows[...] = back_got[...]
    for copy in sent:
        copy.wait_send()


def exchange(pieces, w_in, w_out, key_own, q_send):
    dma = pltpu.SemaphoreType.DMA
    sems = [
        (7,), (2, 4), (2, 8), (8,), (4,),
        (4, 7), (4, 7), (4,), (4, 2, 4), (3,), (7,),
        (7,), (1,), (7,), (3,), (7,), (3,),
    ]
    vmem = pl.BlockSpec(memory_space=pltpu.VMEM)
    consts = constants()
    return pl.pallas_call(
        kernel,
        out_shape=(
            jax.ShapeDtypeStruct((8, 32, 128), BF),
            jax.ShapeDtypeStruct((4, 8, 16, 512), BF),
        ),
        in_specs=[vmem] * (5 + len(consts)),
        out_specs=(vmem, vmem),
        scratch_shapes=[
            pltpu.VMEM((8, 32, 128), BF),
            pltpu.VMEM((4, 2, 8, 32, 1024), BF),
            pltpu.VMEM((4, 8, 64, 128), BF),
            pltpu.VMEM((4, 7, 64, 128), BF),
            pltpu.VMEM((4, 8, 32, 128), BF),
            pltpu.VMEM((4, 2, 8, 32, 896), BF),
            pltpu.VMEM((4, 8, 32, 896), BF),
            pltpu.VMEM((4, 2, 4, 32, 896), BF),
            pltpu.VMEM((4, 2, 4, 32, 896), BF),
            pltpu.VMEM((4, 32, 896), BF),
            pltpu.VMEM((3, 32, 896), BF),
            pltpu.VMEM((8, 32, 128), BF),
            pltpu.VMEM((8, 32, 128), BF),
            pltpu.VMEM((2, 8, 32, 512), BF),
            pltpu.VMEM((8, 4, 16, 128), BF),
            pltpu.VMEM((4, 8, 16, 128), BF),
            pltpu.VMEM((4, 8, 16, 512), BF),
            pltpu.VMEM((8, 4, 16, 512), BF),
            pltpu.VMEM((4, 8, 16, 512), BF),
        ]
        + [dma(shape) for shape in sems for _ in range(2)],
        compiler_params=pltpu.CompilerParams(
            collective_id=0, has_side_effects=True, vmem_limit_bytes=48 * 1024 * 1024
        ),
        cost_estimate=pl.CostEstimate(
            flops=6_000_000_000, bytes_accessed=8_000_000, transcendentals=500_000
        ),
    )(pieces, w_in, w_out, key_own, q_send, *consts)


def on_device(
    query_nope,
    query_rope,
    latent_cache,
    key_rope,
    lengths,
    key_weight,
    expert_input,
    route_slots,
    route_gates,
    trainer_gate_up,
    trainer_down,
    trainer_order,
    rollout_order,
):
    named = route_slots[:, :, None] == jnp.arange(8, dtype=jnp.int32)[None, None, :]
    expert = jnp.sum(jnp.where(named, rollout_order[None, None, :], 0), axis=2)
    one_hot = (expert[:, :, None] == trainer_order[None, None, :]).astype(F32)
    high = lax.reduce_precision(route_gates, 8, 7)
    middle = lax.reduce_precision(route_gates - high, 8, 7)
    low = lax.reduce_precision(route_gates - high - middle, 8, 7)
    gates = jnp.stack([high, middle, low], axis=2).reshape(4, 6)
    routing = jnp.concatenate(
        [one_hot.reshape(4, 16), gates, jnp.zeros((4, 106), F32)], axis=1
    ).astype(BF)
    pieces = expert_input.reshape(4, 8, 7, 128).transpose(1, 2, 0, 3)
    routing = jnp.broadcast_to(routing[None, None], (8, 1, 4, 128))
    pieces = jnp.concatenate([pieces, routing], axis=1).reshape(8, 32, 128)
    q_send = query_nope.reshape(4, NX, NY, 4, NOPE).transpose(2, 1, 0, 3, 4).reshape(8, 4, 16, 128)
    out_rows, latent = exchange(
        pieces,
        trainer_gate_up.reshape(512, 896),
        trainer_down.reshape(256, 896),
        key_weight.reshape(32, 512),
        q_send,
    )
    expert_output = (
        out_rows.reshape(8, 8, 4, 128)[:, :7].transpose(2, 0, 1, 3).reshape(4, 7168)
    )
    query_latent = latent.reshape(32, 4, 4, 512).transpose(1, 0, 2, 3).reshape(4, 128, 512)

    score_scale = 1.0 / math.sqrt(NOPE + ROPE)
    scores = jnp.einsum("rhk,rlk->rhl", query_latent, latent_cache, preferred_element_type=F32)
    scores = scores + jnp.einsum(
        "rhp,rlp->rhl", query_rope, key_rope, preferred_element_type=F32
    )
    scores = scores * score_scale
    visible = (
        jnp.arange(latent_cache.shape[1], dtype=jnp.int32)[None, None, :] < lengths[:, None, None]
    )
    scores = jnp.where(visible, scores, -jnp.inf)
    highest = jnp.max(scores, axis=2, keepdims=True)
    raised = jnp.exp(scores - highest)
    attention = (raised / jnp.sum(raised, axis=2, keepdims=True)).astype(BF)
    latent_output = jnp.einsum(
        "rhl,rlk->rhk", attention, latent_cache, preferred_element_type=F32
    ).astype(BF)
    return (latent_output, expert_output)


def solution(mesh):
    in_specs = (
        P(("dp", "expert"), None, None),
        P(("dp", "expert"), None, None),
        P(("dp", "expert"), None, None),
        P(("dp", "expert"), None, None),
        P(("dp", "expert")),
        P("expert", "dp", None),
        P(("dp", "expert"), None),
        P(("dp", "expert"), None),
        P(("dp", "expert"), None),
        P(None, "expert", None, "dp"),
        P(None, "expert", "dp"),
        P(),
        P(),
    )
    out_specs = (P(("dp", "expert"), None, None), P(("dp", "expert"), None))
    return jax.shard_map(
        on_device, mesh=mesh, in_specs=in_specs, out_specs=out_specs, check_vma=False
    )
```

```python
import math

import jax
import jax.numpy as jnp
import numpy as np
from jax import lax
from jax.experimental import pallas as pl
from jax.experimental.pallas import tpu as pltpu
from jax.sharding import PartitionSpec as P

NOPE = 128
ROPE = 64
NX, NY, NZ = 4, 8, 8
BF = jnp.bfloat16
F32 = jnp.float32
MESH = pl.DeviceIdType.MESH
SCORE_SCALE = 1.0 / math.sqrt(NOPE + ROPE)
X_ORDER = (0, 1, 3, 2)
FORWARD_PLUS = (0, 2, 5, 7)
FORWARD_MINUS = (1, 3, 4, 6)


def constants():
    perm = np.zeros((256, 256), np.float32)
    for z in range(8):
        for t in range(8):
            for r in range(4):
                perm[t * 32 + z * 4 + r, z * 32 + t * 4 + r] = 1
    col = np.arange(512)
    mask_in = np.zeros((128, 1024), np.float32)
    pick = np.zeros((1024, 128), np.float32)
    for k in range(2):
        mask_in[k * 8 + col // 64, k * 512 + col] = 1
        pick[k * 512 + col, (col % 2) * 64 + k * 32 + (col % 64) // 2] = 1
    gate = np.zeros((128, 128), np.float32)
    for k in range(2):
        for j in range(3):
            gate[16 + 3 * k + j, k * 32 : k * 32 + 32] = 1
    spread = np.zeros((2, 128, 512), np.float32)
    mask_out = np.zeros((128, 512), np.float32)
    unit = np.arange(256)
    for k in range(2):
        mask_out[k * 8 + unit // 32, k * 256 + unit] = 1
        for c in range(2):
            spread[c, c * 64 + k * 32 + unit % 32, k * 256 + unit] = 1
    repeat = np.zeros((128, 512), np.float32)
    repeat[((col // 32) % 8) * 16 + col % 16, col] = 1
    by_row = np.zeros((512, 512), np.float32)
    by_row[((col // 4) % 4) * 128 + (col // 16) * 4 + col % 4, col] = 1
    return [
        jnp.asarray(a, BF)
        for a in (perm, perm.T, mask_in, pick, gate, spread, mask_out, repeat, by_row)
    ]


def dot(a, b):
    return jnp.dot(a, b, preferred_element_type=F32)


def dot_nt(a, b):
    return lax.dot_general(a, b, (((1,), (1,)), ((), ())), preferred_element_type=F32)


def kernel(
    x_hbm, slots_hbm, gates_hbm, trainer_hbm, rollout_hbm, w_raw_hbm, w_out_hbm, key_hbm, q_hbm,
    cache_hbm, q_rope_hbm, k_rope_hbm, lengths_hbm,
    perm_hbm, perm_t_hbm, mask_in_hbm, pick_hbm, gate_hbm, spread_hbm, mask_out_hbm, repeat_hbm,
    by_row_hbm,
    out_rows, out_latent,
    x_in, slots, gates, trainer, rollout, w_raw, w_out, key_own, q_send,
    cache, q_rope, k_rope, lengths,
    perm, perm_t, mask_in, pick, gate, spread, mask_out, repeat, by_row,
    pieces, w_in, lat_rows, s_load,
    got, rows, part, part_got, hid, share, share_sib, ring_out, ring_in, col_sum, col_got,
    back_out, back_got, keys, q_col, q_own, lat_own, lat_col, lat_got,
    s_piece, r_piece, s_ring, r_ring, s_x, r_x, s_fwd, r_fwd, s_sib, r_sib,
    s_part, r_part, s_hid, r_hid, s_ssib, r_ssib, s_red, r_red, s_col, r_col, s_back, r_back,
    s_key, r_key, s_ksib, r_ksib, s_qy, r_qy, s_qx, r_qx, s_ly, r_ly, s_lx, r_lx,
):
    z = lax.axis_index("dp")
    e = lax.axis_index("expert")
    c = lax.rem(e, 2)
    y = lax.rem(e // 2, NY)
    x = e // (2 * NY)
    sign = 1 - 2 * c

    def at_z(d):
        return lax.rem(z + d, NZ)

    def at_x(d):
        return lax.rem(x + d, NX)

    def at_y(d):
        return lax.rem(y + NY + d, NY)

    def on_z(d):
        return (at_z(d), e)

    def on_x(d):
        return (z, (at_x(d) * NY + y) * 2 + c)

    def on_y(d):
        return (z, (x * NY + at_y(d)) * 2 + c)

    sibling = (z, e + 1 - 2 * c)

    loads = [
        pltpu.make_async_copy(src, dst, s_load.at[i])
        for i, (src, dst) in enumerate(
            (
                (x_hbm, x_in), (slots_hbm, slots), (gates_hbm, gates),
                (trainer_hbm, trainer), (rollout_hbm, rollout),
                (key_hbm, key_own), (q_hbm, q_send), (perm_hbm, perm),
                (w_raw_hbm, w_raw), (repeat_hbm, repeat),
                (mask_in_hbm, mask_in), (pick_hbm, pick), (gate_hbm, gate),
                (spread_hbm, spread), (mask_out_hbm, mask_out), (w_out_hbm, w_out),
                (perm_t_hbm, perm_t),
                (by_row_hbm, by_row), (lengths_hbm, lengths), (cache_hbm, cache),
                (q_rope_hbm, q_rope), (k_rope_hbm, k_rope),
            )
        )
    ]
    for load in loads:
        load.start()

    barrier = pltpu.get_barrier_semaphore()
    peers = [on_z(d) for d in range(1, NZ)] + [on_y(d) for d in range(1, NY)]
    peers += [on_x(d) for d in range(1, NX)] + [sibling]
    for peer in peers:
        pl.semaphore_signal(barrier, inc=1, device_id=peer, device_id_type=MESH)

    for load in loads[:5]:
        load.wait()
    lane = lax.broadcasted_iota(jnp.int32, (8, 128), 1)
    row = lax.broadcasted_iota(jnp.int32, (8, 128), 0)
    trainer_lane = jnp.zeros((8, 128), jnp.int32)
    for i in range(8):
        trainer_lane = jnp.where(lane % 8 == i, trainer[i], trainer_lane)
    expert = jnp.full((8, 128), -1, jnp.int32)
    gate_lane = jnp.zeros((8, 128), F32)
    for r in range(4):
        for k in range(2):
            expert = jnp.where((row == r) & (lane // 8 == k), rollout[slots[k, r]], expert)
            term = (lane >= 16 + 3 * k) & (lane < 19 + 3 * k)
            gate_lane = jnp.where((row == r) & term, gates[k, r], gate_lane)
    high = gate_lane.astype(BF).astype(F32)
    middle = (gate_lane - high).astype(BF).astype(F32)
    low = gate_lane - high - middle
    term = (lane + 2) % 3
    routing = jnp.where(expert == trainer_lane, 1.0, 0.0)
    routing = routing + jnp.where(term == 0, high, jnp.where(term == 1, middle, low))
    own_rows = x_in[...].astype(F32)
    for d in range(NZ):
        tiles = [own_rows[d * 28 : (d + 1) * 28], routing[0:4]]
        pieces[d] = jnp.concatenate(tiles, axis=0).astype(BF)
    pl.semaphore_wait(barrier, len(peers))

    sent = []

    def send(src, dst, s_sem, r_sem, peer):
        copy = pltpu.make_async_remote_copy(
            src_ref=src, dst_ref=dst, send_sem=s_sem, recv_sem=r_sem,
            device_id=peer, device_id_type=MESH,
        )
        copy.start()
        sent.append(copy)
        return copy

    piece = [
        send(pieces.at[at_z(d)], got.at[z], s_piece.at[d - 1], r_piece.at[d - 1], on_z(d))
        for d in range(1, NZ)
    ]
    loads[6].wait()
    q_y = [
        send(q_send.at[at_y(d)], q_col.at[y], s_qy.at[d - 1], r_qy.at[d - 1], on_y(d))
        for d in range(1, NY)
    ]
    got[z] = pieces[z]
    q_col[y] = q_send[y]
    loads[5].wait()
    keys[c, z] = key_own[...]

    loads[7].wait()
    for copy in piece:
        copy.wait_recv()
    turned = dot(perm[...], got[...].reshape(256, 128)).astype(BF)
    for t in range(8):
        rows[x, c, y, :, t * 128 : (t + 1) * 128] = turned[t * 32 : (t + 1) * 32]

    def block(xi, yi):
        return rows.at[xi, c, yi]

    origins, x_plus, x_minus, far = [], [], [], []

    def to_x(origin):
        k = len(origins)
        origins.append(origin)
        b = block(x, origin)
        x_plus.append(send(b, b, s_x.at[0, k], r_x.at[0, k], on_x(1)))
        x_minus.append(send(b, b, s_x.at[1, k], r_x.at[1, k], on_x(3)))

    def pass_on(k):
        x_minus[k].wait_recv()
        if k in FORWARD_MINUS:
            b = block(at_x(1), origins[k])
            far.append(send(b, b, s_fwd.at[k], r_fwd.at[k], on_x(3)))
        x_plus[k].wait_recv()
        if k in FORWARD_PLUS:
            b = block(at_x(3), origins[k])
            far.append(send(b, b, s_fwd.at[k], r_fwd.at[k], on_x(1)))

    def ring(origin, way, step):
        b = block(x, origin)
        peer = on_y(sign) if way == 0 else on_y(-sign)
        return send(b, b, s_ring.at[way, step], r_ring.at[way, step], peer)

    plus, minus = ring(y, 0, 0), ring(y, 1, 0)
    to_x(y)
    key_z = [
        send(key_own, keys.at[c, z], s_key.at[d - 1], r_key.at[d - 1], on_z(d))
        for d in range(1, NZ)
    ]
    for copy in q_y:
        copy.wait_recv()
    q_x = [
        send(q_col.at[:, at_x(d)], q_own.at[x], s_qx.at[d - 1], r_qx.at[d - 1], on_x(d))
        for d in range(1, NX)
    ]
    q_own[x] = q_col[:, x]
    for step in range(1, 5):
        plus.wait_recv()
        origin = at_y(-sign * step)
        if step < 4:
            plus = ring(origin, 0, step)
        to_x(origin)
        if step < 4:
            minus.wait_recv()
            origin = at_y(sign * step)
            if step < 3:
                minus = ring(origin, 1, step)
            to_x(origin)
        if step == 1:
            loads[8].wait()

            def line_up(i, carry):
                start = pl.multiple_of(i * 64, 64)
                w_in[pl.ds(start, 64), :] = w_raw[i].reshape(64, 896)
                return carry

            lax.fori_loop(0, 8, line_up, 0)
        if step == 2:
            for load in loads[9:]:
                load.wait()
            pass_on(0)
        if step == 3:
            pass_on(1)
            pass_on(2)
            for copy in key_z:
                copy.wait_recv()
            key_sib = send(keys.at[c], keys.at[c], s_ksib.at[0], r_ksib.at[0], sibling)

    def to_sibling(j):
        b = rows.at[at_x(X_ORDER[j]), c]
        return send(b, b, s_sib.at[j], r_sib.at[j], sibling)

    def project(group):
        for j in group:
            xi = at_x(X_ORDER[j])

            def body(ci, carry):
                routing = rows[xi, ci, :, :, 896:1024].reshape(256, 128)
                mask = dot(routing, mask_in[...])
                values = dot_nt(rows[xi, ci, :, :, 0:896].reshape(256, 896), w_in[...])
                first = (values * mask[:, :512]).astype(BF)
                second = (values * mask[:, 512:]).astype(BF)
                picked = dot(first, pick[0:512, :]) + dot(second, pick[512:1024, :])
                picked = picked.astype(BF).reshape(8, 32, 128)
                part[:, j, pl.ds(pl.multiple_of(ci * 32, 32), 32), :] = picked
                return carry

            lax.fori_loop(0, 2, body, 0)
        js = pl.ds(group[0], len(group))
        return [
            send(
                part.at[at_z(d), js], part_got.at[d - 1, js],
                s_part.at[group[0], d - 1], r_part.at[group[0], d - 1], on_z(d),
            )
            for d in range(1, NZ)
        ]

    def activate(group, arriving):
        for copy in arriving:
            copy.wait_recv()
        for j in group:
            xi = at_x(X_ORDER[j])
            total = part[z, j].astype(F32)
            for d in range(7):
                total = total + part_got[d, j].astype(F32)
            up = pltpu.roll(total, 64, 1)
            routing = rows[xi, :, z, :, 896:1024].reshape(64, 128)
            value = total / (1.0 + jnp.exp(-total)) * up * dot(routing, gate[...])
            lane = lax.broadcasted_iota(jnp.int32, (32, 128), 1)
            packed = jnp.where(lane < 64, value[0:32], pltpu.roll(value[32:64], 64, 1))
            hid[z, j] = packed.astype(BF)
        js = pl.ds(group[0], len(group))
        return [
            send(
                hid.at[z, js], hid.at[z, js],
                s_hid.at[group[0], d - 1], r_hid.at[group[0], d - 1], on_z(d),
            )
            for d in range(1, NZ)
        ]

    def project_down(group, arriving):
        for copy in arriving:
            copy.wait_recv()
        copies = []
        for j in group:
            xi = at_x(X_ORDER[j])

            def body(i, carry):
                ci = lax.rem(1 - c + i, 2)
                routing = rows[xi, ci, :, :, 896:1024].reshape(256, 128)
                wide = dot(hid[:, j].reshape(256, 128), spread[ci]) * dot(routing, mask_out[...])
                dense = (wide[:, :256] + wide[:, 256:]).astype(BF)
                share[j, ci] = dot(dense, w_out[...]).astype(BF).reshape(8, 32, 896)
                return carry

            lax.fori_loop(0, 2, body, 0)
            copies.append(
                send(share.at[j, 1 - c], share_sib.at[j], s_ssib.at[j], r_ssib.at[j], sibling)
            )
        return copies

    def own_share(j, target):
        return share[j, c, target].astype(F32) + share_sib[j, target].astype(F32)

    def reduce_step(group, step, state):
        new = [None, None]
        if step == 1:
            for copy in state:
                copy.wait_recv()
        js = pl.ds(group[0], len(group))
        for way, hops in ((0, 4), (1, 3)):
            if step > hops:
                new[way] = state[way]
                continue
            target = at_y(sign * (hops + 1 - step) * (1 - 2 * way))
            if step > 1:
                state[way].wait_recv()
            for j in group:
                value = own_share(j, target)
                if step > 1:
                    value = value + ring_in[way, step - 2, j].astype(F32)
                ring_out[way, step - 1, j] = value.astype(BF)
            new[way] = send(
                ring_out.at[way, step - 1, js], ring_in.at[way, step - 1, js],
                s_red.at[group[0], way, step - 1], r_red.at[group[0], way, step - 1],
                on_y(sign * (1 - 2 * way)),
            )
        return new

    def reduce_end(group, state):
        state[0].wait_recv()
        state[1].wait_recv()
        copies = []
        for j in group:
            value = own_share(j, y) + ring_in[0, 3, j].astype(F32) + ring_in[1, 2, j].astype(F32)
            col_sum[j] = value.astype(BF)
            if j > 0:
                copies.append(
                    send(
                        col_sum.at[j], col_got.at[j - 1],
                        s_col.at[j - 1], r_col.at[j - 1], on_x(X_ORDER[j]),
                    )
                )
        return copies

    def absorb():
        for copy in q_x:
            copy.wait_recv()
        key_sib.wait_recv()
        wide = dot(q_own[...].reshape(512, 128), repeat[...])
        row = lax.broadcasted_iota(jnp.int32, (512, 512), 0)
        lane = lax.broadcasted_iota(jnp.int32, (512, 512), 1)
        head = (lane // 256) * 2 + (lane // 16) % 2
        wide = jnp.where(row % 4 == head, wide, 0.0).astype(BF)
        lat_own[...] = dot(wide, keys[...].reshape(512, 512)).astype(BF).reshape(4, 8, 16, 512)
        copies = [
            send(lat_own.at[:, at_y(d)], lat_col.at[y], s_ly.at[d - 1], r_ly.at[d - 1], on_y(d))
            for d in range(1, NY)
        ]
        lat_col[y] = lat_own[:, y]
        return copies

    def latent_x(arriving):
        for copy in arriving:
            copy.wait_recv()
        copies = [
            send(lat_col.at[:, at_x(d)], lat_got.at[x], s_lx.at[d - 1], r_lx.at[d - 1], on_x(d))
            for d in range(1, NX)
        ]
        lat_got[x] = lat_col[:, x]
        return copies

    def latent_end(arriving):
        for copy in arriving:
            copy.wait_recv()
        turned = dot(by_row[...], lat_got[...].reshape(512, 512)).astype(BF)
        lat_rows[...] = turned.reshape(4, 128, 512)

    def attend(r):
        scores = dot_nt(lat_rows[r], cache[r])
        scores = scores + lax.dot_general(
            q_rope[r], k_rope[r], (((0,), (0,)), ((), ())), preferred_element_type=F32
        )
        scores = scores * SCORE_SCALE
        place = lax.broadcasted_iota(jnp.int32, (128, 512), 1)
        scores = jnp.where(place < lengths[r], scores, -jnp.inf)
        raised = jnp.exp(scores - jnp.max(scores, axis=1, keepdims=True))
        attention = (raised / jnp.sum(raised, axis=1, keepdims=True)).astype(BF)
        out_latent[r] = dot(attention, cache[r]).astype(BF)

    one, two, three = (0,), (1, 2), (3,)
    sib = [to_sibling(0)]
    lat_y = absorb()
    sib[0].wait_recv()
    part_1 = project(one)
    for k in range(3, 8):
        pass_on(k)
    sib.append(to_sibling(1))
    sib.append(to_sibling(2))
    sib[1].wait_recv()
    sib[2].wait_recv()
    part_2 = project(two)
    hid_1 = activate(one, part_1)
    for copy in far:
        copy.wait_recv()
    sib.append(to_sibling(3))
    sib[3].wait_recv()
    part_3 = project(three)
    down_1 = project_down(one, hid_1)
    hid_2 = activate(two, part_2)
    lat_x = latent_x(lat_y)
    red_1 = reduce_step(one, 1, down_1)
    hid_3 = activate(three, part_3)
    down_2 = project_down(two, hid_2)
    red_1 = reduce_step(one, 2, red_1)
    down_3 = project_down(three, hid_3)
    red_2 = reduce_step(two, 1, down_2)
    red_1 = reduce_step(one, 3, red_1)
    red_3 = reduce_step(three, 1, down_3)
    red_1 = reduce_step(one, 4, red_1)
    latent_end(lat_x)
    red_2 = reduce_step(two, 2, red_2)
    red_3 = reduce_step(three, 2, red_3)
    attend(0)
    red_2 = reduce_step(two, 3, red_2)
    red_3 = reduce_step(three, 3, red_3)
    reduce_end(one, red_1)
    attend(1)
    red_2 = reduce_step(two, 4, red_2)
    red_3 = reduce_step(three, 4, red_3)
    attend(2)
    cols = reduce_end(two, red_2)
    cols += reduce_end(three, red_3)
    attend(3)

    total = col_sum[0].astype(F32)
    for j in range(3):
        cols[j].wait_recv()
        total = total + col_got[j].astype(F32)
    total = total.astype(BF)
    tiles = [total[:, t * 128 : (t + 1) * 128] for t in range(7)] + [jnp.zeros((32, 128), BF)]
    tiles = jnp.concatenate(tiles, axis=0)
    back_out[...] = dot(perm_t[...], tiles).astype(BF).reshape(8, 32, 128)
    back = [
        send(back_out.at[at_z(d)], back_got.at[z], s_back.at[d - 1], r_back.at[d - 1], on_z(d))
        for d in range(1, NZ)
    ]
    back_got[z] = back_out[z]
    for copy in back:
        copy.wait_recv()
    for d in range(NZ):
        part_rows = back_got[d].astype(F32)
        for t in range(7):
            first = (d * 7 + t) * 128
            out_rows[:, first : first + 128] = part_rows[t * 4 : t * 4 + 4].astype(BF)
    for copy in sent:
        copy.wait_send()


def exchange(*operands):
    dma = pltpu.SemaphoreType.DMA
    sems = [
        (7,), (2, 4), (2, 8), (8,), (4,),
        (4, 7), (4, 7), (4,), (4, 2, 4), (3,), (7,),
        (7,), (1,), (7,), (3,), (7,), (3,),
    ]
    vmem = pl.BlockSpec(memory_space=pltpu.VMEM)
    operands = list(operands) + constants()
    smem = (1, 2, 3, 4, 12)
    landing = [
        (pltpu.SMEM if i in smem else pltpu.VMEM)(a.shape, a.dtype) for i, a in enumerate(operands)
    ]
    return pl.pallas_call(
        kernel,
        out_shape=(
            jax.ShapeDtypeStruct((4, 7168), BF),
            jax.ShapeDtypeStruct((4, 128, 512), BF),
        ),
        in_specs=[pl.BlockSpec(memory_space=pltpu.HBM)] * len(operands),
        out_specs=(vmem, vmem),
        scratch_shapes=landing
        + [
            pltpu.VMEM((8, 32, 128), BF),
            pltpu.VMEM((512, 896), BF),
            pltpu.VMEM((4, 128, 512), BF),
            dma((len(operands),)),
            pltpu.VMEM((8, 32, 128), BF),
            pltpu.VMEM((4, 2, 8, 32, 1024), BF),
            pltpu.VMEM((8, 4, 64, 128), BF),
            pltpu.VMEM((7, 4, 64, 128), BF),
            pltpu.VMEM((8, 4, 32, 128), BF),
            pltpu.VMEM((4, 2, 8, 32, 896), BF),
            pltpu.VMEM((4, 8, 32, 896), BF),
            pltpu.VMEM((2, 4, 4, 32, 896), BF),
            pltpu.VMEM((2, 4, 4, 32, 896), BF),
            pltpu.VMEM((4, 32, 896), BF),
            pltpu.VMEM((3, 32, 896), BF),
            pltpu.VMEM((8, 32, 128), BF),
            pltpu.VMEM((8, 32, 128), BF),
            pltpu.VMEM((2, 8, 32, 512), BF),
            pltpu.VMEM((8, 4, 16, 128), BF),
            pltpu.VMEM((4, 8, 16, 128), BF),
            pltpu.VMEM((4, 8, 16, 512), BF),
            pltpu.VMEM((8, 4, 16, 512), BF),
            pltpu.VMEM((4, 8, 16, 512), BF),
        ]
        + [dma(shape) for shape in sems for _ in range(2)],
        compiler_params=pltpu.CompilerParams(
            collective_id=0, has_side_effects=True, vmem_limit_bytes=60 * 1024 * 1024
        ),
        cost_estimate=pl.CostEstimate(
            flops=6_000_000_000, bytes_accessed=8_000_000, transcendentals=500_000
        ),
    )(*operands)


def on_device(
    query_nope,
    query_rope,
    latent_cache,
    key_rope,
    lengths,
    key_weight,
    expert_input,
    route_slots,
    route_gates,
    trainer_gate_up,
    trainer_down,
    trainer_order,
    rollout_order,
):
    q_send = query_nope.reshape(4, NX, NY, 4, NOPE).transpose(2, 1, 0, 3, 4).reshape(8, 4, 16, 128)
    expert_output, latent_output = exchange(
        expert_input.reshape(4, 56, 128).transpose(1, 0, 2).reshape(224, 128),
        route_slots.T,
        route_gates.T,
        trainer_order,
        rollout_order,
        trainer_gate_up,
        trainer_down.reshape(256, 896),
        key_weight.reshape(32, 512),
        q_send,
        latent_cache,
        query_rope.transpose(0, 2, 1),
        key_rope.transpose(0, 2, 1),
        lengths,
    )
    return (latent_output, expert_output)


def solution(mesh):
    in_specs = (
        P(("dp", "expert"), None, None),
        P(("dp", "expert"), None, None),
        P(("dp", "expert"), None, None),
        P(("dp", "expert"), None, None),
        P(("dp", "expert")),
        P("expert", "dp", None),
        P(("dp", "expert"), None),
        P(("dp", "expert"), None),
        P(("dp", "expert"), None),
        P(None, "expert", None, "dp"),
        P(None, "expert", "dp"),
        P(),
        P(),
    )
    out_specs = (P(("dp", "expert"), None, None), P(("dp", "expert"), None))
    return jax.shard_map(
        on_device, mesh=mesh, in_specs=in_specs, out_specs=out_specs, check_vma=False
    )
```

```python
import math

import jax
import jax.numpy as jnp
import numpy as np
from jax import lax
from jax.experimental import pallas as pl
from jax.experimental.pallas import tpu as pltpu
from jax.sharding import PartitionSpec as P

NOPE = 128
ROPE = 64
NX, NY, NZ = 4, 8, 8
BF = jnp.bfloat16
F32 = jnp.float32
MESH = pl.DeviceIdType.MESH
SCORE_SCALE = 1.0 / math.sqrt(NOPE + ROPE)
X_ORDER = (0, 1, 3, 2)
NEAR_FIRST = (1, 7, 2, 6, 3, 5, 4)
FAR_FIRST = (4, 3, 5, 2, 6, 1, 7)
FORWARD_PLUS = (0, 2, 5, 7)
FORWARD_MINUS = (1, 3, 4, 6)


def constants():
    perm = np.zeros((256, 256), np.float32)
    for z in range(8):
        for t in range(8):
            for r in range(4):
                perm[t * 32 + z * 4 + r, z * 32 + t * 4 + r] = 1
    col = np.arange(512)
    mask_in = np.zeros((128, 1024), np.float32)
    pick = np.zeros((1024, 128), np.float32)
    for k in range(2):
        mask_in[k * 8 + col // 64, k * 512 + col] = 1
        pick[k * 512 + col, (col % 2) * 64 + k * 32 + (col % 64) // 2] = 1
    gate = np.zeros((128, 128), np.float32)
    for k in range(2):
        for j in range(3):
            gate[16 + 3 * k + j, k * 32 : k * 32 + 32] = 1
    spread = np.zeros((2, 128, 512), np.float32)
    mask_out = np.zeros((128, 512), np.float32)
    unit = np.arange(256)
    for k in range(2):
        mask_out[k * 8 + unit // 32, k * 256 + unit] = 1
        for c in range(2):
            spread[c, c * 64 + k * 32 + unit % 32, k * 256 + unit] = 1
    repeat = np.zeros((128, 512), np.float32)
    repeat[((col // 32) % 8) * 16 + col % 16, col] = 1
    by_row = np.zeros((512, 512), np.float32)
    by_row[((col // 4) % 4) * 128 + (col // 16) * 4 + col % 4, col] = 1
    return [
        jnp.asarray(a, BF)
        for a in (perm, perm.T, mask_in, pick, gate, spread, mask_out, repeat, by_row)
    ]


def dot(a, b):
    return jnp.dot(a, b, preferred_element_type=F32)


def dot_nt(a, b):
    return lax.dot_general(a, b, (((1,), (1,)), ((), ())), preferred_element_type=F32)


def kernel(
    x_hbm, slots_hbm, gates_hbm, trainer_hbm, rollout_hbm, w_raw_hbm, w_out_hbm, key_hbm, q_hbm,
    cache_hbm, q_rope_hbm, k_rope_hbm, lengths_hbm,
    perm_hbm, perm_t_hbm, mask_in_hbm, pick_hbm, gate_hbm, spread_hbm, mask_out_hbm, repeat_hbm,
    by_row_hbm,
    out_rows, out_latent,
    x_in, slots, gates, trainer, rollout, w_raw, w_out, key_own, q_in,
    cache, q_rope, k_rope, lengths,
    perm, perm_t, mask_in, pick, gate, spread, mask_out, repeat, by_row,
    pieces, w_in, lat_rows, q_send, s_load,
    got, rows, part, part_got, hid, share, share_sib, ring_out, ring_in,
    back_out, back_got, keys, q_col, q_own, lat_own, lat_col, lat_got,
    s_piece, r_piece, s_ring, r_ring, s_x, r_x, s_fwd, r_fwd, s_sib, r_sib,
    s_part, r_part, s_hid, r_hid, s_ssib, r_ssib, s_red, r_red, s_back, r_back,
    s_key, r_key, s_ksib, r_ksib, s_qy, r_qy, s_qx, r_qx, s_ly, r_ly, s_lx, r_lx,
):
    z = lax.axis_index("dp")
    e = lax.axis_index("expert")
    c = lax.rem(e, 2)
    y = lax.rem(e // 2, NY)
    x = e // (2 * NY)
    sign = 1 - 2 * c

    def at_z(d):
        return lax.rem(z + d, NZ)

    def at_x(d):
        return lax.rem(x + d, NX)

    def at_y(d):
        return lax.rem(y + NY + d, NY)

    def on_z(d):
        return (at_z(d), e)

    def on_x(d):
        return (z, (at_x(d) * NY + y) * 2 + c)

    def on_xz(dx, dz):
        return (at_z(dz), (at_x(dx) * NY + y) * 2 + c)

    def on_y(d):
        return (z, (x * NY + at_y(d)) * 2 + c)

    sibling = (z, e + 1 - 2 * c)

    loads = [
        pltpu.make_async_copy(src, dst, s_load.at[i])
        for i, (src, dst) in enumerate(
            (
                (x_hbm, x_in), (slots_hbm, slots), (gates_hbm, gates),
                (trainer_hbm, trainer), (rollout_hbm, rollout),
                (key_hbm, key_own), (q_hbm, q_in), (perm_hbm, perm),
                (w_raw_hbm, w_raw), (repeat_hbm, repeat),
                (mask_in_hbm, mask_in), (pick_hbm, pick), (gate_hbm, gate),
                (spread_hbm, spread), (mask_out_hbm, mask_out), (w_out_hbm, w_out),
                (perm_t_hbm, perm_t),
                (by_row_hbm, by_row), (lengths_hbm, lengths), (cache_hbm, cache),
                (q_rope_hbm, q_rope), (k_rope_hbm, k_rope),
            )
        )
    ]
    for load in loads:
        load.start()

    barrier = pltpu.get_barrier_semaphore()
    peers = [on_z(d) for d in range(1, NZ)] + [on_y(d) for d in range(1, NY)]
    peers += [on_xz(dx, dz) for dx in range(1, NX) for dz in range(NZ)] + [sibling]
    for peer in peers:
        pl.semaphore_signal(barrier, inc=1, device_id=peer, device_id_type=MESH)

    for load in loads[:5]:
        load.wait()
    lane = lax.broadcasted_iota(jnp.int32, (8, 128), 1)
    row = lax.broadcasted_iota(jnp.int32, (8, 128), 0)
    trainer_lane = jnp.zeros((8, 128), jnp.int32)
    for i in range(8):
        trainer_lane = jnp.where(lane % 8 == i, trainer[i], trainer_lane)
    expert = jnp.full((8, 128), -1, jnp.int32)
    gate_lane = jnp.zeros((8, 128), F32)
    for r in range(4):
        for k in range(2):
            expert = jnp.where((row == r) & (lane // 8 == k), rollout[slots[k, r]], expert)
            term = (lane >= 16 + 3 * k) & (lane < 19 + 3 * k)
            gate_lane = jnp.where((row == r) & term, gates[k, r], gate_lane)
    high = gate_lane.astype(BF).astype(F32)
    middle = (gate_lane - high).astype(BF).astype(F32)
    low = gate_lane - high - middle
    term = (lane + 2) % 3
    routing = jnp.where(expert == trainer_lane, 1.0, 0.0)
    routing = routing + jnp.where(term == 0, high, jnp.where(term == 1, middle, low))
    own_rows = x_in[...].astype(F32)
    for d in range(NZ):
        tiles = [own_rows[d * 28 : (d + 1) * 28], routing[0:4]]
        pieces[d] = jnp.concatenate(tiles, axis=0).astype(BF)
    pl.semaphore_wait(barrier, len(peers))

    sent = []

    def send(src, dst, s_sem, r_sem, peer):
        copy = pltpu.make_async_remote_copy(
            src_ref=src, dst_ref=dst, send_sem=s_sem, recv_sem=r_sem,
            device_id=peer, device_id_type=MESH,
        )
        copy.start()
        sent.append(copy)
        return copy

    piece = [
        send(pieces.at[at_z(d)], got.at[z], s_piece.at[d - 1], r_piece.at[d - 1], on_z(d))
        for d in FAR_FIRST
    ]
    loads[6].wait()
    loads[17].wait()
    turned = lax.dot_general(
        by_row[...], q_in[...], (((0,), (0,)), ((), ())), preferred_element_type=F32
    )
    q_send[...] = turned.astype(BF).reshape(4, 8, 16, 128)
    q_y = [
        send(q_send.at[:, at_y(d)], q_col.at[y], s_qy.at[d - 1], r_qy.at[d - 1], on_y(d))
        for d in FAR_FIRST
    ]
    got[z] = pieces[z]
    q_col[y] = q_send[:, y]
    loads[5].wait()
    keys[c, z] = key_own[...]

    loads[7].wait()
    for copy in piece:
        copy.wait_recv()
    turned = dot(perm[...], got[...].reshape(256, 128)).astype(BF)
    for t in range(8):
        rows[x, c, y, :, t * 128 : (t + 1) * 128] = turned[t * 32 : (t + 1) * 32]

    def block(xi, yi):
        return rows.at[xi, c, yi]

    origins, x_plus, x_minus, far = [], [], [], []

    def to_x(origin):
        k = len(origins)
        origins.append(origin)
        b = block(x, origin)
        x_plus.append(send(b, b, s_x.at[0, k], r_x.at[0, k], on_x(1)))
        x_minus.append(send(b, b, s_x.at[1, k], r_x.at[1, k], on_x(3)))

    def pass_on(k):
        x_minus[k].wait_recv()
        if k in FORWARD_MINUS:
            b = block(at_x(1), origins[k])
            far.append(send(b, b, s_fwd.at[k], r_fwd.at[k], on_x(3)))
        x_plus[k].wait_recv()
        if k in FORWARD_PLUS:
            b = block(at_x(3), origins[k])
            far.append(send(b, b, s_fwd.at[k], r_fwd.at[k], on_x(1)))

    own = block(x, y)
    y_copies = [
        send(own, own, s_ring.at[i], r_ring.at[i], on_y(sign * d))
        for i, d in enumerate((1, -1, 2, -2))
    ]
    to_x(y)
    key_z = [
        send(key_own, keys.at[c, z], s_key.at[d - 1], r_key.at[d - 1], on_z(d))
        for d in FAR_FIRST
    ]
    for copy in q_y:
        copy.wait_recv()
    q_x = [
        send(q_col.at[:, at_x(d)], q_own.at[x], s_qx.at[d - 1], r_qx.at[d - 1], on_x(d))
        for d in range(1, NX)
    ]
    q_own[x] = q_col[:, x]
    loads[8].wait()

    def line_up(i, carry):
        start = pl.multiple_of(i * 64, 64)
        w_in[pl.ds(start, 64), :] = w_raw[i].reshape(64, 896)
        return carry

    for step, d in enumerate((-1, 1, -2, 2, -3, 3, -4)):
        y_copies[step].wait_recv()
        b = block(x, at_y(sign * d))
        if d == -2:
            y_copies.append(send(b, b, s_ring.at[4], r_ring.at[4], on_y(sign)))
            far_y = send(b, b, s_ring.at[6], r_ring.at[6], on_y(2 * sign))
        if d == 2:
            y_copies.append(send(b, b, s_ring.at[5], r_ring.at[5], on_y(-sign)))
            y_copies.append(far_y)
        to_x(at_y(sign * d))
        if step == 1:
            lax.fori_loop(0, 8, line_up, 0)
        if step == 3:
            for load in loads[9:17] + loads[18:]:
                load.wait()
        if step == 5:
            for k in range(3):
                pass_on(k)
            for copy in key_z:
                copy.wait_recv()
            key_sib = send(keys.at[c], keys.at[c], s_ksib.at[0], r_ksib.at[0], sibling)

    def to_sibling(j):
        b = rows.at[at_x(X_ORDER[j]), c]
        return send(b, b, s_sib.at[j], r_sib.at[j], sibling)

    def project(group):
        for j in group:
            xi = at_x(X_ORDER[j])

            def body(ci, carry):
                routing = rows[xi, ci, :, :, 896:1024].reshape(256, 128)
                mask = dot(routing, mask_in[...])
                values = dot_nt(rows[xi, ci, :, :, 0:896].reshape(256, 896), w_in[...])
                first = (values * mask[:, :512]).astype(BF)
                second = (values * mask[:, 512:]).astype(BF)
                picked = dot(first, pick[0:512, :]) + dot(second, pick[512:1024, :])
                picked = picked.astype(BF).reshape(8, 32, 128)
                part[:, j, pl.ds(pl.multiple_of(ci * 32, 32), 32), :] = picked
                return carry

            lax.fori_loop(0, 2, body, 0)
        js = pl.ds(group[0], len(group))
        return [
            send(
                part.at[at_z(d), js], part_got.at[d - 1, js],
                s_part.at[group[0], d - 1], r_part.at[group[0], d - 1], on_z(d),
            )
            for d in FAR_FIRST
        ]

    def activate(group, arriving):
        for copy in arriving:
            copy.wait_recv()
        for j in group:
            xi = at_x(X_ORDER[j])
            total = part[z, j].astype(F32)
            for d in range(7):
                total = total + part_got[d, j].astype(F32)
            up = pltpu.roll(total, 64, 1)
            routing = rows[xi, :, z, :, 896:1024].reshape(64, 128)
            value = total / (1.0 + jnp.exp(-total)) * up * dot(routing, gate[...])
            lane = lax.broadcasted_iota(jnp.int32, (32, 128), 1)
            packed = jnp.where(lane < 64, value[0:32], pltpu.roll(value[32:64], 64, 1))
            hid[z, j] = packed.astype(BF)
        js = pl.ds(group[0], len(group))
        return [
            send(
                hid.at[z, js], hid.at[z, js],
                s_hid.at[group[0], d - 1], r_hid.at[group[0], d - 1], on_z(d),
            )
            for d in FAR_FIRST
        ]

    def project_down(group, arriving):
        for copy in arriving:
            copy.wait_recv()
        copies = []
        for j in group:
            xi = at_x(X_ORDER[j])

            def body(i, carry):
                ci = lax.rem(1 - c + i, 2)
                routing = rows[xi, ci, :, :, 896:1024].reshape(256, 128)
                wide = dot(hid[:, j].reshape(256, 128), spread[ci]) * dot(routing, mask_out[...])
                dense = (wide[:, :256] + wide[:, 256:]).astype(BF)
                share[j, ci] = dot(dense, w_out[...]).astype(BF).reshape(8, 32, 896)
                return carry

            lax.fori_loop(0, 2, body, 0)
            copies.append(
                send(share.at[j, 1 - c], share_sib.at[j], s_ssib.at[j], r_ssib.at[j], sibling)
            )
        return copies

    def own_share(j, target):
        return share[j, c, target].astype(F32) + share_sib[j, target].astype(F32)

    def move_sum(group, i, offset, to, arrived):
        js = pl.ds(group[0], len(group))
        target = at_y(sign * offset)
        for j in group:
            value = own_share(j, target)
            for k in arrived:
                value = value + ring_in[k, j].astype(F32)
            ring_out[i, j] = value.astype(BF)
        return send(
            ring_out.at[i, js], ring_in.at[i, js],
            s_red.at[group[0], i], r_red.at[group[0], i], on_y(sign * to),
        )

    def reduce_first(group, arriving):
        for copy in arriving:
            copy.wait_recv()
        hops = ((4, 3), (3, 2), (-3, -2), (2, 1), (-2, -1))
        return [move_sum(group, i, offset, to, ()) for i, (offset, to) in enumerate(hops)]

    def reduce_second(group, arriving):
        for i in (4, 2):
            arriving[i].wait_recv()
        copies = [move_sum(group, 6, -1, -1, (2, 4))]
        for i in (3, 1, 0):
            arriving[i].wait_recv()
        return copies + [move_sum(group, 5, 1, 1, (0, 1, 3))]

    def ring_step(group, step, state):
        if step == 1:
            for copy in state:
                copy.wait_recv()
        new = [None, None]
        for way, hops in ((0, 4), (1, 3)):
            if step > hops:
                new[way] = state[way]
                continue
            arrived = ()
            if step > 1:
                state[way].wait_recv()
                arrived = (way * 4 + step - 2,)
            toward = 1 - 2 * way
            new[way] = move_sum(
                group, way * 4 + step - 1, toward * (hops + 1 - step), toward, arrived
            )
        return new

    def reduce_end(group, arriving, last=(5, 6)):
        for copy in arriving:
            copy.wait_recv()
        copies = []
        for j in group:
            value = own_share(j, y)
            for k in last:
                value = value + ring_in[k, j].astype(F32)
            value = value.astype(BF)
            tiles = [value[:, t * 128 : (t + 1) * 128] for t in range(7)]
            tiles = jnp.concatenate(tiles + [jnp.zeros((32, 128), BF)], axis=0)
            back_out[j] = dot(perm_t[...], tiles).astype(BF).reshape(8, 32, 128)
            for d in FAR_FIRST + (0,):
                if j == 0 and d == 0:
                    back_got[j, z] = back_out[j, z]
                    continue
                copies.append(
                    send(
                        back_out.at[j, at_z(d)], back_got.at[j, z],
                        s_back.at[j, d], r_back.at[j, d], on_xz(X_ORDER[j], d),
                    )
                )
        return copies

    def absorb():
        for copy in q_x:
            copy.wait_recv()
        key_sib.wait_recv()
        wide = dot(q_own[...].reshape(512, 128), repeat[...])
        row = lax.broadcasted_iota(jnp.int32, (512, 512), 0)
        lane = lax.broadcasted_iota(jnp.int32, (512, 512), 1)
        head = (lane // 256) * 2 + (lane // 16) % 2
        wide = jnp.where(row % 4 == head, wide, 0.0).astype(BF)
        lat_own[...] = dot(wide, keys[...].reshape(512, 512)).astype(BF).reshape(4, 8, 16, 512)
        copies = [
            send(lat_own.at[:, at_y(d)], lat_col.at[y], s_ly.at[d - 1], r_ly.at[d - 1], on_y(d))
            for d in FAR_FIRST
        ]
        lat_col[y] = lat_own[:, y]
        return copies

    def latent_x(arriving):
        for copy in arriving:
            copy.wait_recv()
        copies = [
            send(lat_col.at[:, at_x(d)], lat_got.at[x], s_lx.at[d - 1], r_lx.at[d - 1], on_x(d))
            for d in range(1, NX)
        ]
        lat_got[x] = lat_col[:, x]
        return copies

    def latent_end(arriving):
        for copy in arriving:
            copy.wait_recv()
        turned = dot(by_row[...], lat_got[...].reshape(512, 512)).astype(BF)
        lat_rows[...] = turned.reshape(4, 128, 512)

    def attend(r):
        scores = dot_nt(lat_rows[r], cache[r])
        scores = scores + lax.dot_general(
            q_rope[r], k_rope[r], (((0,), (0,)), ((), ())), preferred_element_type=F32
        )
        scores = scores * SCORE_SCALE
        place = lax.broadcasted_iota(jnp.int32, (128, 512), 1)
        scores = jnp.where(place < lengths[r], scores, -jnp.inf)
        raised = jnp.exp(scores - jnp.max(scores, axis=1, keepdims=True))
        attention = (raised / jnp.sum(raised, axis=1, keepdims=True)).astype(BF)
        out_latent[r] = dot(attention, cache[r]).astype(BF)

    one, two, three = (0,), (1, 2), (3,)
    sib = [to_sibling(0)]
    sib[0].wait_recv()
    part_1 = project(one)
    lat_y = absorb()
    for k in range(3, 8):
        pass_on(k)
    sib.append(to_sibling(1))
    sib.append(to_sibling(2))
    sib[1].wait_recv()
    sib[2].wait_recv()
    part_2 = project(two)
    for copy in far:
        copy.wait_recv()
    sib.append(to_sibling(3))
    hid_1 = activate(one, part_1)
    sib[3].wait_recv()
    part_3 = project(three)
    sums_1 = project_down(one, hid_1)
    hid_2 = activate(two, part_2)
    sums_1 = ring_step(one, 1, sums_1)
    hid_3 = activate(three, part_3)
    sums_1 = ring_step(one, 2, sums_1)
    lat_x = latent_x(lat_y)
    sums_2 = project_down(two, hid_2)
    sums_1 = ring_step(one, 3, sums_1)
    sums_3 = project_down(three, hid_3)
    sums_2 = ring_step(two, 1, sums_2)
    sums_3 = ring_step(three, 1, sums_3)
    sums_1 = ring_step(one, 4, sums_1)
    latent_end(lat_x)
    sums_2 = ring_step(two, 2, sums_2)
    sums_3 = ring_step(three, 2, sums_3)
    attend(0)
    sums_2 = ring_step(two, 3, sums_2)
    sums_3 = ring_step(three, 3, sums_3)
    backs = reduce_end(one, sums_1, (3, 6))
    attend(1)
    sums_2 = ring_step(two, 4, sums_2)
    sums_3 = ring_step(three, 4, sums_3)
    attend(2)
    backs += reduce_end(two, sums_2, (3, 6))
    backs += reduce_end(three, sums_3, (3, 6))
    attend(3)

    for copy in backs:
        copy.wait_recv()
    for d in range(NZ):
        total = back_got[0, d].astype(F32)
        for j in range(1, NX):
            total = total + back_got[j, d].astype(F32)
        for t in range(7):
            first = (d * 7 + t) * 128
            out_rows[:, first : first + 128] = total[t * 4 : t * 4 + 4].astype(BF)
    for copy in sent:
        copy.wait_send()


def exchange(*operands):
    dma = pltpu.SemaphoreType.DMA
    sems = [
        (7,), (7,), (2, 8), (8,), (4,),
        (4, 7), (4, 7), (4,), (4, 7), (4, 8),
        (7,), (1,), (7,), (3,), (7,), (3,),
    ]
    vmem = pl.BlockSpec(memory_space=pltpu.VMEM)
    operands = list(operands) + constants()
    smem = (1, 2, 3, 4, 12)
    landing = [
        (pltpu.SMEM if i in smem else pltpu.VMEM)(a.shape, a.dtype) for i, a in enumerate(operands)
    ]
    return pl.pallas_call(
        kernel,
        out_shape=(
            jax.ShapeDtypeStruct((4, 7168), BF),
            jax.ShapeDtypeStruct((4, 128, 512), BF),
        ),
        in_specs=[pl.BlockSpec(memory_space=pltpu.HBM)] * len(operands),
        out_specs=(vmem, vmem),
        scratch_shapes=landing
        + [
            pltpu.VMEM((8, 32, 128), BF),
            pltpu.VMEM((512, 896), BF),
            pltpu.VMEM((4, 128, 512), BF),
            pltpu.VMEM((4, 8, 16, 128), BF),
            dma((len(operands),)),
            pltpu.VMEM((8, 32, 128), BF),
            pltpu.VMEM((4, 2, 8, 32, 1024), BF),
            pltpu.VMEM((8, 4, 64, 128), BF),
            pltpu.VMEM((7, 4, 64, 128), BF),
            pltpu.VMEM((8, 4, 32, 128), BF),
            pltpu.VMEM((4, 2, 8, 32, 896), BF),
            pltpu.VMEM((4, 8, 32, 896), BF),
            pltpu.VMEM((7, 4, 32, 896), BF),
            pltpu.VMEM((7, 4, 32, 896), BF),
            pltpu.VMEM((4, 8, 32, 128), BF),
            pltpu.VMEM((4, 8, 32, 128), BF),
            pltpu.VMEM((2, 8, 32, 512), BF),
            pltpu.VMEM((8, 4, 16, 128), BF),
            pltpu.VMEM((4, 8, 16, 128), BF),
            pltpu.VMEM((4, 8, 16, 512), BF),
            pltpu.VMEM((8, 4, 16, 512), BF),
            pltpu.VMEM((4, 8, 16, 512), BF),
        ]
        + [dma(shape) for shape in sems for _ in range(2)],
        compiler_params=pltpu.CompilerParams(
            collective_id=0, has_side_effects=True, vmem_limit_bytes=60 * 1024 * 1024
        ),
        cost_estimate=pl.CostEstimate(
            flops=6_000_000_000, bytes_accessed=8_000_000, transcendentals=500_000
        ),
    )(*operands)


def place(rows, latent):
    def body(rows_in, latent_in, rows_out, latent_out):
        rows_out[...] = rows_in[...]
        latent_out[...] = latent_in[...]

    vmem = pl.BlockSpec(memory_space=pltpu.VMEM)
    return pl.pallas_call(
        body,
        out_shape=tuple(jax.ShapeDtypeStruct(a.shape, a.dtype) for a in (rows, latent)),
        in_specs=[vmem, vmem],
        out_specs=(vmem, vmem),
    )(rows, latent)


def on_device(
    query_nope,
    query_rope,
    latent_cache,
    key_rope,
    lengths,
    key_weight,
    expert_input,
    route_slots,
    route_gates,
    trainer_gate_up,
    trainer_down,
    trainer_order,
    rollout_order,
):
    expert_output, latent_output = exchange(
        expert_input.reshape(4, 56, 128).transpose(1, 0, 2).reshape(224, 128),
        route_slots.T,
        route_gates.T,
        trainer_order,
        rollout_order,
        trainer_gate_up,
        trainer_down.reshape(256, 896),
        key_weight.reshape(32, 512),
        query_nope.reshape(512, 128),
        latent_cache,
        query_rope.transpose(0, 2, 1),
        key_rope.transpose(0, 2, 1),
        lengths,
    )
    expert_output, latent_output = place(expert_output, latent_output)
    return (latent_output, expert_output)


def solution(mesh):
    in_specs = (
        P(("dp", "expert"), None, None),
        P(("dp", "expert"), None, None),
        P(("dp", "expert"), None, None),
        P(("dp", "expert"), None, None),
        P(("dp", "expert")),
        P("expert", "dp", None),
        P(("dp", "expert"), None),
        P(("dp", "expert"), None),
        P(("dp", "expert"), None),
        P(None, "expert", None, "dp"),
        P(None, "expert", "dp"),
        P(),
        P(),
    )
    out_specs = (P(("dp", "expert"), None, None), P(("dp", "expert"), None))
    return jax.shard_map(
        on_device, mesh=mesh, in_specs=in_specs, out_specs=out_specs, check_vma=False
    )
```

```python
import math

import jax
import jax.numpy as jnp
import numpy as np
from jax import lax
from jax.experimental import pallas as pl
from jax.experimental.pallas import tpu as pltpu
from jax.sharding import PartitionSpec as P

NOPE = 128
ROPE = 64
NX, NY, NZ = 4, 8, 8
BF = jnp.bfloat16
F32 = jnp.float32
MESH = pl.DeviceIdType.MESH
SCORE_SCALE = 1.0 / math.sqrt(NOPE + ROPE)
X_ORDER = (0, 1, 3, 2)
NEAR_FIRST = (1, 7, 2, 6, 3, 5, 4)
FAR_FIRST = (4, 3, 5, 2, 6, 1, 7)
FORWARD_PLUS = (0, 2, 5, 7)
FORWARD_MINUS = (1, 3, 4, 6)


def constants():
    perm = np.zeros((256, 256), np.float32)
    for z in range(8):
        for t in range(8):
            for r in range(4):
                perm[t * 32 + z * 4 + r, z * 32 + t * 4 + r] = 1
    col = np.arange(512)
    mask_in = np.zeros((128, 1024), np.float32)
    pick = np.zeros((1024, 128), np.float32)
    for k in range(2):
        mask_in[k * 8 + col // 64, k * 512 + col] = 1
        pick[k * 512 + col, (col % 2) * 64 + k * 32 + (col % 64) // 2] = 1
    gate = np.zeros((128, 128), np.float32)
    for k in range(2):
        for j in range(3):
            gate[16 + 3 * k + j, k * 32 : k * 32 + 32] = 1
    spread = np.zeros((2, 128, 512), np.float32)
    mask_out = np.zeros((128, 512), np.float32)
    unit = np.arange(256)
    for k in range(2):
        mask_out[k * 8 + unit // 32, k * 256 + unit] = 1
        for c in range(2):
            spread[c, c * 64 + k * 32 + unit % 32, k * 256 + unit] = 1
    repeat = np.zeros((128, 512), np.float32)
    repeat[((col // 32) % 8) * 16 + col % 16, col] = 1
    by_row = np.zeros((512, 512), np.float32)
    by_row[((col // 4) % 4) * 128 + (col // 16) * 4 + col % 4, col] = 1
    return [
        jnp.asarray(a, BF)
        for a in (perm, perm.T, mask_in, pick, gate, spread, mask_out, repeat, by_row)
    ]


def dot(a, b):
    return jnp.dot(a, b, preferred_element_type=F32)


def dot_nt(a, b):
    return lax.dot_general(a, b, (((1,), (1,)), ((), ())), preferred_element_type=F32)


def kernel(
    x_hbm, slots_hbm, gates_hbm, trainer_hbm, rollout_hbm, w_raw_hbm, w_out_hbm, key_hbm, q_hbm,
    cache_hbm, q_rope_hbm, k_rope_hbm, lengths_hbm,
    perm_hbm, perm_t_hbm, mask_in_hbm, pick_hbm, gate_hbm, spread_hbm, mask_out_hbm, repeat_hbm,
    by_row_hbm,
    out_rows, out_latent,
    x_in, slots, gates, trainer, rollout, w_raw, w_out, key_own, q_in,
    cache, q_rope, k_rope, lengths,
    perm, perm_t, mask_in, pick, gate, spread, mask_out, repeat, by_row,
    pieces, w_in, lat_rows, q_send, s_load,
    got, rows, part, part_got, hid, share, share_sib, ring_out, ring_in,
    back_out, back_got, keys, q_col, q_own, lat_own, lat_col, lat_got,
    s_piece, r_piece, s_ring, r_ring, s_x, r_x, s_fwd, r_fwd, s_sib, r_sib,
    s_part, r_part, s_hid, r_hid, s_ssib, r_ssib, s_red, r_red, s_back, r_back,
    s_key, r_key, s_ksib, r_ksib, s_qy, r_qy, s_qx, r_qx, s_ly, r_ly, s_lx, r_lx,
):
    z = lax.axis_index("dp")
    e = lax.axis_index("expert")
    c = lax.rem(e, 2)
    y = lax.rem(e // 2, NY)
    x = e // (2 * NY)
    sign = 1 - 2 * c

    def at_z(d):
        return lax.rem(z + d, NZ)

    def at_x(d):
        return lax.rem(x + d, NX)

    def at_y(d):
        return lax.rem(y + NY + d, NY)

    def on_z(d):
        return (at_z(d), e)

    def on_x(d):
        return (z, (at_x(d) * NY + y) * 2 + c)

    def on_xz(dx, dz):
        return (at_z(dz), (at_x(dx) * NY + y) * 2 + c)

    def on_y(d):
        return (z, (x * NY + at_y(d)) * 2 + c)

    sibling = (z, e + 1 - 2 * c)

    loads = [
        pltpu.make_async_copy(src, dst, s_load.at[i])
        for i, (src, dst) in enumerate(
            (
                (x_hbm, x_in), (slots_hbm, slots), (gates_hbm, gates),
                (trainer_hbm, trainer), (rollout_hbm, rollout),
                (key_hbm, key_own), (q_hbm, q_in), (perm_hbm, perm),
                (w_raw_hbm, w_raw), (repeat_hbm, repeat),
                (mask_in_hbm, mask_in), (pick_hbm, pick), (gate_hbm, gate),
                (spread_hbm, spread), (mask_out_hbm, mask_out), (w_out_hbm, w_out),
                (perm_t_hbm, perm_t),
                (by_row_hbm, by_row), (lengths_hbm, lengths), (cache_hbm, cache),
                (q_rope_hbm, q_rope), (k_rope_hbm, k_rope),
            )
        )
    ]
    for load in loads:
        load.start()

    barrier = pltpu.get_barrier_semaphore()
    peers = [on_z(d) for d in range(1, NZ)] + [on_y(d) for d in range(1, NY)]
    peers += [on_xz(dx, dz) for dx in range(1, NX) for dz in range(NZ)] + [sibling]
    for peer in peers:
        pl.semaphore_signal(barrier, inc=1, device_id=peer, device_id_type=MESH)

    for load in loads[:5]:
        load.wait()
    lane = lax.broadcasted_iota(jnp.int32, (8, 128), 1)
    row = lax.broadcasted_iota(jnp.int32, (8, 128), 0)
    trainer_lane = jnp.zeros((8, 128), jnp.int32)
    for i in range(8):
        trainer_lane = jnp.where(lane % 8 == i, trainer[i], trainer_lane)
    expert = jnp.full((8, 128), -1, jnp.int32)
    gate_lane = jnp.zeros((8, 128), F32)
    for r in range(4):
        for k in range(2):
            expert = jnp.where((row == r) & (lane // 8 == k), rollout[slots[k, r]], expert)
            term = (lane >= 16 + 3 * k) & (lane < 19 + 3 * k)
            gate_lane = jnp.where((row == r) & term, gates[k, r], gate_lane)
    high = gate_lane.astype(BF).astype(F32)
    middle = (gate_lane - high).astype(BF).astype(F32)
    low = gate_lane - high - middle
    term = (lane + 2) % 3
    routing = jnp.where(expert == trainer_lane, 1.0, 0.0)
    routing = routing + jnp.where(term == 0, high, jnp.where(term == 1, middle, low))
    own_rows = x_in[...].astype(F32)
    for d in range(NZ):
        tiles = [own_rows[d * 28 : (d + 1) * 28], routing[0:4]]
        pieces[d] = jnp.concatenate(tiles, axis=0).astype(BF)
    pl.semaphore_wait(barrier, len(peers))

    sent = []

    def send(src, dst, s_sem, r_sem, peer):
        copy = pltpu.make_async_remote_copy(
            src_ref=src, dst_ref=dst, send_sem=s_sem, recv_sem=r_sem,
            device_id=peer, device_id_type=MESH,
        )
        copy.start()
        sent.append(copy)
        return copy

    piece = [
        send(pieces.at[at_z(d)], got.at[z], s_piece.at[d - 1], r_piece.at[d - 1], on_z(d))
        for d in FAR_FIRST
    ]
    loads[6].wait()
    loads[17].wait()
    turned = lax.dot_general(
        by_row[...], q_in[...], (((0,), (0,)), ((), ())), preferred_element_type=F32
    )
    q_send[...] = turned.astype(BF).reshape(4, 8, 16, 128)
    q_y = [
        send(q_send.at[:, at_y(d)], q_col.at[y], s_qy.at[d - 1], r_qy.at[d - 1], on_y(d))
        for d in FAR_FIRST
    ]
    got[z] = pieces[z]
    q_col[y] = q_send[:, y]
    loads[5].wait()
    keys[c, z] = key_own[...]

    loads[7].wait()
    for copy in piece:
        copy.wait_recv()
    turned = dot(perm[...], got[...].reshape(256, 128)).astype(BF)
    for t in range(8):
        rows[x, c, y, :, t * 128 : (t + 1) * 128] = turned[t * 32 : (t + 1) * 32]

    def block(xi, yi):
        return rows.at[xi, c, yi]

    origins, x_plus, x_minus, far = [], [], [], []

    def to_x(origin):
        k = len(origins)
        origins.append(origin)
        b = block(x, origin)
        x_plus.append(send(b, b, s_x.at[0, k], r_x.at[0, k], on_x(1)))
        x_minus.append(send(b, b, s_x.at[1, k], r_x.at[1, k], on_x(3)))

    def pass_on(k):
        x_minus[k].wait_recv()
        if k in FORWARD_MINUS:
            b = block(at_x(1), origins[k])
            far.append(send(b, b, s_fwd.at[k], r_fwd.at[k], on_x(3)))
        x_plus[k].wait_recv()
        if k in FORWARD_PLUS:
            b = block(at_x(3), origins[k])
            far.append(send(b, b, s_fwd.at[k], r_fwd.at[k], on_x(1)))

    own = block(x, y)
    y_copies = [
        send(own, own, s_ring.at[i], r_ring.at[i], on_y(sign * d))
        for i, d in enumerate((1, -1, 2, -2))
    ]
    to_x(y)
    key_z = [
        send(key_own, keys.at[c, z], s_key.at[d - 1], r_key.at[d - 1], on_z(d))
        for d in FAR_FIRST
    ]
    for copy in q_y:
        copy.wait_recv()
    q_x = [
        send(q_col.at[:, at_x(d)], q_own.at[x], s_qx.at[d - 1], r_qx.at[d - 1], on_x(d))
        for d in range(1, NX)
    ]
    q_own[x] = q_col[:, x]
    loads[8].wait()

    def line_up(i, carry):
        start = pl.multiple_of(i * 64, 64)
        w_in[pl.ds(start, 64), :] = w_raw[i].reshape(64, 896)
        return carry

    for step, d in enumerate((-1, 1, -2, 2, -3, 3, -4)):
        y_copies[step].wait_recv()
        b = block(x, at_y(sign * d))
        if d == -2:
            y_copies.append(send(b, b, s_ring.at[4], r_ring.at[4], on_y(sign)))
            far_y = send(b, b, s_ring.at[6], r_ring.at[6], on_y(2 * sign))
        if d == 2:
            y_copies.append(send(b, b, s_ring.at[5], r_ring.at[5], on_y(-sign)))
            y_copies.append(far_y)
        to_x(at_y(sign * d))
        if step == 1:
            lax.fori_loop(0, 8, line_up, 0)
        if step == 3:
            for load in loads[9:17] + loads[18:]:
                load.wait()
        if step == 5:
            for k in range(3):
                pass_on(k)
            for copy in key_z:
                copy.wait_recv()
            key_sib = send(keys.at[c], keys.at[c], s_ksib.at[0], r_ksib.at[0], sibling)

    def to_sibling(j):
        b = rows.at[at_x(X_ORDER[j]), c]
        return send(b, b, s_sib.at[j], r_sib.at[j], sibling)

    def project(group):
        for j in group:
            xi = at_x(X_ORDER[j])

            def body(ci, carry):
                routing = rows[xi, ci, :, :, 896:1024].reshape(256, 128)
                mask = dot(routing, mask_in[...])
                values = dot_nt(rows[xi, ci, :, :, 0:896].reshape(256, 896), w_in[...])
                first = (values * mask[:, :512]).astype(BF)
                second = (values * mask[:, 512:]).astype(BF)
                picked = dot(first, pick[0:512, :]) + dot(second, pick[512:1024, :])
                picked = picked.astype(BF).reshape(8, 32, 128)
                part[:, j, pl.ds(pl.multiple_of(ci * 32, 32), 32), :] = picked
                return carry

            lax.fori_loop(0, 2, body, 0)
        js = pl.ds(group[0], len(group))
        return [
            send(
                part.at[at_z(d), js], part_got.at[d - 1, js],
                s_part.at[group[0], d - 1], r_part.at[group[0], d - 1], on_z(d),
            )
            for d in FAR_FIRST
        ]

    def activate(group, arriving):
        for copy in arriving:
            copy.wait_recv()
        for j in group:
            xi = at_x(X_ORDER[j])
            total = part[z, j].astype(F32)
            for d in range(7):
                total = total + part_got[d, j].astype(F32)
            up = pltpu.roll(total, 64, 1)
            routing = rows[xi, :, z, :, 896:1024].reshape(64, 128)
            value = total / (1.0 + jnp.exp(-total)) * up * dot(routing, gate[...])
            lane = lax.broadcasted_iota(jnp.int32, (32, 128), 1)
            packed = jnp.where(lane < 64, value[0:32], pltpu.roll(value[32:64], 64, 1))
            hid[z, j] = packed.astype(BF)
        js = pl.ds(group[0], len(group))
        return [
            send(
                hid.at[z, js], hid.at[z, js],
                s_hid.at[group[0], d - 1], r_hid.at[group[0], d - 1], on_z(d),
            )
            for d in FAR_FIRST
        ]

    def project_down(group, arriving):
        for copy in arriving:
            copy.wait_recv()
        copies = []
        for j in group:
            xi = at_x(X_ORDER[j])

            def body(i, carry):
                ci = lax.rem(1 - c + i, 2)
                routing = rows[xi, ci, :, :, 896:1024].reshape(256, 128)
                wide = dot(hid[:, j].reshape(256, 128), spread[ci]) * dot(routing, mask_out[...])
                dense = (wide[:, :256] + wide[:, 256:]).astype(BF)
                share[j, ci] = dot(dense, w_out[...]).astype(BF).reshape(8, 32, 896)
                return carry

            lax.fori_loop(0, 2, body, 0)
            copies.append(
                send(share.at[j, 1 - c], share_sib.at[j], s_ssib.at[j], r_ssib.at[j], sibling)
            )
        return copies

    def own_share(j, target):
        return share[j, c, target].astype(F32) + share_sib[j, target].astype(F32)

    def move_sum(group, i, offset, to, arrived):
        js = pl.ds(group[0], len(group))
        target = at_y(sign * offset)
        for j in group:
            value = own_share(j, target)
            for k in arrived:
                value = value + ring_in[k, j].astype(F32)
            ring_out[i, j] = value.astype(BF)
        return send(
            ring_out.at[i, js], ring_in.at[i, js],
            s_red.at[group[0], i], r_red.at[group[0], i], on_y(sign * to),
        )

    def reduce_first(group, arriving):
        for copy in arriving:
            copy.wait_recv()
        hops = ((4, 3), (3, 2), (-3, -2), (2, 1), (-2, -1))
        return [move_sum(group, i, offset, to, ()) for i, (offset, to) in enumerate(hops)]

    def reduce_second(group, arriving):
        for i in (4, 2):
            arriving[i].wait_recv()
        copies = [move_sum(group, 6, -1, -1, (2, 4))]
        for i in (3, 1, 0):
            arriving[i].wait_recv()
        return copies + [move_sum(group, 5, 1, 1, (0, 1, 3))]

    def ring_step(group, step, state):
        if step == 1:
            for copy in state:
                copy.wait_recv()
        new = [None, None]
        for way, hops in ((0, 4), (1, 3)):
            if step > hops:
                new[way] = state[way]
                continue
            arrived = ()
            if step > 1:
                state[way].wait_recv()
                arrived = (way * 4 + step - 2,)
            toward = 1 - 2 * way
            new[way] = move_sum(
                group, way * 4 + step - 1, toward * (hops + 1 - step), toward, arrived
            )
        return new

    def reduce_end(group, arriving, last=(5, 6)):
        for copy in arriving:
            copy.wait_recv()
        copies = []
        for j in group:
            value = own_share(j, y)
            for k in last:
                value = value + ring_in[k, j].astype(F32)
            value = value.astype(BF)
            tiles = [value[:, t * 128 : (t + 1) * 128] for t in range(7)]
            tiles = jnp.concatenate(tiles + [jnp.zeros((32, 128), BF)], axis=0)
            back_out[j] = dot(perm_t[...], tiles).astype(BF).reshape(8, 32, 128)
            for d in FAR_FIRST + (0,):
                if j == 0 and d == 0:
                    back_got[j, z] = back_out[j, z]
                    continue
                copies.append(
                    send(
                        back_out.at[j, at_z(d)], back_got.at[j, z],
                        s_back.at[j, d], r_back.at[j, d], on_xz(X_ORDER[j], d),
                    )
                )
        return copies

    def absorb():
        for copy in q_x:
            copy.wait_recv()
        key_sib.wait_recv()
        wide = dot(q_own[...].reshape(512, 128), repeat[...])
        row = lax.broadcasted_iota(jnp.int32, (512, 512), 0)
        lane = lax.broadcasted_iota(jnp.int32, (512, 512), 1)
        head = (lane // 256) * 2 + (lane // 16) % 2
        wide = jnp.where(row % 4 == head, wide, 0.0).astype(BF)
        lat_own[...] = dot(wide, keys[...].reshape(512, 512)).astype(BF).reshape(4, 8, 16, 512)
        copies = [
            send(lat_own.at[:, at_y(d)], lat_col.at[y], s_ly.at[d - 1], r_ly.at[d - 1], on_y(d))
            for d in FAR_FIRST
        ]
        lat_col[y] = lat_own[:, y]
        return copies

    def latent_x(arriving):
        for copy in arriving:
            copy.wait_recv()
        copies = [
            send(lat_col.at[:, at_x(d)], lat_got.at[x], s_lx.at[d - 1], r_lx.at[d - 1], on_x(d))
            for d in range(1, NX)
        ]
        lat_got[x] = lat_col[:, x]
        return copies

    def latent_end(arriving):
        for copy in arriving:
            copy.wait_recv()
        turned = dot(by_row[...], lat_got[...].reshape(512, 512)).astype(BF)
        lat_rows[...] = turned.reshape(4, 128, 512)

    def attend(r):
        scores = dot_nt(lat_rows[r], cache[r])
        scores = scores + lax.dot_general(
            q_rope[r], k_rope[r], (((0,), (0,)), ((), ())), preferred_element_type=F32
        )
        scores = scores * SCORE_SCALE
        place = lax.broadcasted_iota(jnp.int32, (128, 512), 1)
        scores = jnp.where(place < lengths[r], scores, -jnp.inf)
        raised = jnp.exp(scores - jnp.max(scores, axis=1, keepdims=True))
        attention = (raised / jnp.sum(raised, axis=1, keepdims=True)).astype(BF)
        out_latent[r] = dot(attention, cache[r]).astype(BF)

    one, two, three = (0,), (1, 2), (3,)
    sib = [to_sibling(0)]
    sib[0].wait_recv()
    part_1 = project(one)
    lat_y = absorb()
    for k in range(3, 8):
        pass_on(k)
    sib.append(to_sibling(1))
    sib.append(to_sibling(2))
    hid_1 = activate(one, part_1)
    sib[1].wait_recv()
    sib[2].wait_recv()
    part_2 = project(two)
    for copy in far:
        copy.wait_recv()
    sib.append(to_sibling(3))
    sums_1 = project_down(one, hid_1)
    sib[3].wait_recv()
    part_3 = project(three)
    sums_1 = ring_step(one, 1, sums_1)
    hid_2 = activate(two, part_2)
    lat_x = latent_x(lat_y)
    sums_1 = ring_step(one, 2, sums_1)
    hid_3 = activate(three, part_3)
    sums_1 = ring_step(one, 3, sums_1)
    sums_2 = project_down(two, hid_2)
    sums_1 = ring_step(one, 4, sums_1)
    sums_3 = project_down(three, hid_3)
    sums_2 = ring_step(two, 1, sums_2)
    sums_3 = ring_step(three, 1, sums_3)
    backs = reduce_end(one, sums_1, (3, 6))
    latent_end(lat_x)
    sums_2 = ring_step(two, 2, sums_2)
    sums_3 = ring_step(three, 2, sums_3)
    attend(0)
    sums_2 = ring_step(two, 3, sums_2)
    sums_3 = ring_step(three, 3, sums_3)
    attend(1)
    sums_2 = ring_step(two, 4, sums_2)
    sums_3 = ring_step(three, 4, sums_3)
    attend(2)
    backs += reduce_end(two, sums_2, (3, 6))
    backs += reduce_end(three, sums_3, (3, 6))
    attend(3)

    for copy in backs:
        copy.wait_recv()
    for d in range(NZ):
        total = back_got[0, d].astype(F32)
        for j in range(1, NX):
            total = total + back_got[j, d].astype(F32)
        for t in range(7):
            first = (d * 7 + t) * 128
            out_rows[:, first : first + 128] = total[t * 4 : t * 4 + 4].astype(BF)
    for copy in sent:
        copy.wait_send()


def exchange(*operands):
    dma = pltpu.SemaphoreType.DMA
    sems = [
        (7,), (7,), (2, 8), (8,), (4,),
        (4, 7), (4, 7), (4,), (4, 7), (4, 8),
        (7,), (1,), (7,), (3,), (7,), (3,),
    ]
    vmem = pl.BlockSpec(memory_space=pltpu.VMEM)
    operands = list(operands) + constants()
    smem = (1, 2, 3, 4, 12)
    landing = [
        (pltpu.SMEM if i in smem else pltpu.VMEM)(a.shape, a.dtype) for i, a in enumerate(operands)
    ]
    return pl.pallas_call(
        kernel,
        out_shape=(
            jax.ShapeDtypeStruct((4, 7168), BF),
            jax.ShapeDtypeStruct((4, 128, 512), BF),
        ),
        in_specs=[pl.BlockSpec(memory_space=pltpu.HBM)] * len(operands),
        out_specs=(vmem, vmem),
        scratch_shapes=landing
        + [
            pltpu.VMEM((8, 32, 128), BF),
            pltpu.VMEM((512, 896), BF),
            pltpu.VMEM((4, 128, 512), BF),
            pltpu.VMEM((4, 8, 16, 128), BF),
            dma((len(operands),)),
            pltpu.VMEM((8, 32, 128), BF),
            pltpu.VMEM((4, 2, 8, 32, 1024), BF),
            pltpu.VMEM((8, 4, 64, 128), BF),
            pltpu.VMEM((7, 4, 64, 128), BF),
            pltpu.VMEM((8, 4, 32, 128), BF),
            pltpu.VMEM((4, 2, 8, 32, 896), BF),
            pltpu.VMEM((4, 8, 32, 896), BF),
            pltpu.VMEM((7, 4, 32, 896), BF),
            pltpu.VMEM((7, 4, 32, 896), BF),
            pltpu.VMEM((4, 8, 32, 128), BF),
            pltpu.VMEM((4, 8, 32, 128), BF),
            pltpu.VMEM((2, 8, 32, 512), BF),
            pltpu.VMEM((8, 4, 16, 128), BF),
            pltpu.VMEM((4, 8, 16, 128), BF),
            pltpu.VMEM((4, 8, 16, 512), BF),
            pltpu.VMEM((8, 4, 16, 512), BF),
            pltpu.VMEM((4, 8, 16, 512), BF),
        ]
        + [dma(shape) for shape in sems for _ in range(2)],
        compiler_params=pltpu.CompilerParams(
            collective_id=0, has_side_effects=True, vmem_limit_bytes=60 * 1024 * 1024
        ),
        cost_estimate=pl.CostEstimate(
            flops=6_000_000_000, bytes_accessed=8_000_000, transcendentals=500_000
        ),
    )(*operands)


def place(rows, latent):
    def body(rows_in, latent_in, rows_out, latent_out):
        rows_out[...] = rows_in[...]
        latent_out[...] = latent_in[...]

    vmem = pl.BlockSpec(memory_space=pltpu.VMEM)
    return pl.pallas_call(
        body,
        out_shape=tuple(jax.ShapeDtypeStruct(a.shape, a.dtype) for a in (rows, latent)),
        in_specs=[vmem, vmem],
        out_specs=(vmem, vmem),
    )(rows, latent)


def on_device(
    query_nope,
    query_rope,
    latent_cache,
    key_rope,
    lengths,
    key_weight,
    expert_input,
    route_slots,
    route_gates,
    trainer_gate_up,
    trainer_down,
    trainer_order,
    rollout_order,
):
    expert_output, latent_output = exchange(
        expert_input.reshape(4, 56, 128).transpose(1, 0, 2).reshape(224, 128),
        route_slots.T,
        route_gates.T,
        trainer_order,
        rollout_order,
        trainer_gate_up,
        trainer_down.reshape(256, 896),
        key_weight.reshape(32, 512),
        query_nope.reshape(512, 128),
        latent_cache,
        query_rope.transpose(0, 2, 1),
        key_rope.transpose(0, 2, 1),
        lengths,
    )
    expert_output, latent_output = place(expert_output, latent_output)
    return (latent_output, expert_output)


def solution(mesh):
    in_specs = (
        P(("dp", "expert"), None, None),
        P(("dp", "expert"), None, None),
        P(("dp", "expert"), None, None),
        P(("dp", "expert"), None, None),
        P(("dp", "expert")),
        P("expert", "dp", None),
        P(("dp", "expert"), None),
        P(("dp", "expert"), None),
        P(("dp", "expert"), None),
        P(None, "expert", None, "dp"),
        P(None, "expert", "dp"),
        P(),
        P(),
    )
    out_specs = (P(("dp", "expert"), None, None), P(("dp", "expert"), None))
    return jax.shard_map(
        on_device, mesh=mesh, in_specs=in_specs, out_specs=out_specs, check_vma=False
    )
```

```python
import math

import jax
import jax.numpy as jnp
import numpy as np
from jax import lax
from jax.experimental import pallas as pl
from jax.experimental.pallas import tpu as pltpu
from jax.sharding import PartitionSpec as P

NOPE = 128
ROPE = 64
NX, NY, NZ = 4, 8, 8
BF = jnp.bfloat16
F32 = jnp.float32
MESH = pl.DeviceIdType.MESH
SCORE_SCALE = 1.0 / math.sqrt(NOPE + ROPE)
X_ORDER = (0, 1, 3, 2)
NEAR_FIRST = (1, 7, 2, 6, 3, 5, 4)
FAR_FIRST = (4, 3, 5, 2, 6, 1, 7)
FORWARD_PLUS = (0, 2, 5, 7)
FORWARD_MINUS = (1, 3, 4, 6)


def constants():
    perm = np.zeros((256, 256), np.float32)
    for z in range(8):
        for t in range(8):
            for r in range(4):
                perm[t * 32 + z * 4 + r, z * 32 + t * 4 + r] = 1
    col = np.arange(512)
    mask_in = np.zeros((128, 1024), np.float32)
    pick = np.zeros((1024, 128), np.float32)
    for k in range(2):
        mask_in[k * 8 + col // 64, k * 512 + col] = 1
        pick[k * 512 + col, (col % 2) * 64 + k * 32 + (col % 64) // 2] = 1
    gate = np.zeros((128, 128), np.float32)
    for k in range(2):
        for j in range(3):
            gate[16 + 3 * k + j, k * 32 : k * 32 + 32] = 1
    spread = np.zeros((2, 128, 512), np.float32)
    mask_out = np.zeros((128, 512), np.float32)
    unit = np.arange(256)
    for k in range(2):
        mask_out[k * 8 + unit // 32, k * 256 + unit] = 1
        for c in range(2):
            spread[c, c * 64 + k * 32 + unit % 32, k * 256 + unit] = 1
    repeat = np.zeros((128, 512), np.float32)
    repeat[((col // 32) % 8) * 16 + col % 16, col] = 1
    by_row = np.zeros((512, 512), np.float32)
    by_row[((col // 4) % 4) * 128 + (col // 16) * 4 + col % 4, col] = 1
    return [
        jnp.asarray(a, BF)
        for a in (perm, perm.T, mask_in, pick, gate, spread, mask_out, repeat, by_row)
    ]


def dot(a, b):
    return jnp.dot(a, b, preferred_element_type=F32)


def dot_nt(a, b):
    return lax.dot_general(a, b, (((1,), (1,)), ((), ())), preferred_element_type=F32)


def kernel(
    x_hbm, slots_hbm, gates_hbm, trainer_hbm, rollout_hbm, w_raw_hbm, w_out_hbm, key_hbm, q_hbm,
    cache_hbm, q_rope_hbm, k_rope_hbm, lengths_hbm,
    perm_hbm, perm_t_hbm, mask_in_hbm, pick_hbm, gate_hbm, spread_hbm, mask_out_hbm, repeat_hbm,
    by_row_hbm,
    out_rows, out_latent,
    x_in, slots, gates, trainer, rollout, w_raw, w_out, key_own, q_in,
    cache, q_rope, k_rope, lengths,
    perm, perm_t, mask_in, pick, gate, spread, mask_out, repeat, by_row,
    pieces, w_in, lat_rows, q_send, s_load,
    got, rows, part, part_got, hid, share, share_sib, ring_out, ring_in,
    back_out, back_got, keys, q_col, q_own, lat_own, lat_col, lat_got,
    s_piece, r_piece, s_ring, r_ring, s_x, r_x, s_fwd, r_fwd, s_sib, r_sib,
    s_part, r_part, s_hid, r_hid, s_ssib, r_ssib, s_red, r_red, s_back, r_back,
    s_key, r_key, s_ksib, r_ksib, s_qy, r_qy, s_qx, r_qx, s_ly, r_ly, s_lx, r_lx,
):
    z = lax.axis_index("dp")
    e = lax.axis_index("expert")
    c = lax.rem(e, 2)
    y = lax.rem(e // 2, NY)
    x = e // (2 * NY)
    sign = 1 - 2 * c

    def at_z(d):
        return lax.rem(z + d, NZ)

    def at_x(d):
        return lax.rem(x + d, NX)

    def at_y(d):
        return lax.rem(y + NY + d, NY)

    def on_z(d):
        return (at_z(d), e)

    def on_x(d):
        return (z, (at_x(d) * NY + y) * 2 + c)

    def on_xz(dx, dz):
        return (at_z(dz), (at_x(dx) * NY + y) * 2 + c)

    def on_y(d):
        return (z, (x * NY + at_y(d)) * 2 + c)

    sibling = (z, e + 1 - 2 * c)

    loads = [
        pltpu.make_async_copy(src, dst, s_load.at[i])
        for i, (src, dst) in enumerate(
            (
                (x_hbm, x_in), (slots_hbm, slots), (gates_hbm, gates),
                (trainer_hbm, trainer), (rollout_hbm, rollout),
                (key_hbm, key_own), (q_hbm, q_in), (perm_hbm, perm),
                (w_raw_hbm, w_raw), (repeat_hbm, repeat),
                (mask_in_hbm, mask_in), (pick_hbm, pick), (gate_hbm, gate),
                (spread_hbm, spread), (mask_out_hbm, mask_out), (w_out_hbm, w_out),
                (perm_t_hbm, perm_t),
                (by_row_hbm, by_row), (lengths_hbm, lengths), (cache_hbm, cache),
                (q_rope_hbm, q_rope), (k_rope_hbm, k_rope),
            )
        )
    ]
    for load in loads:
        load.start()

    barrier = pltpu.get_barrier_semaphore()
    peers = [on_z(d) for d in range(1, NZ)] + [on_y(d) for d in range(1, NY)]
    peers += [on_xz(dx, dz) for dx in range(1, NX) for dz in range(NZ)] + [sibling]
    for peer in peers:
        pl.semaphore_signal(barrier, inc=1, device_id=peer, device_id_type=MESH)

    for load in loads[:5]:
        load.wait()
    lane = lax.broadcasted_iota(jnp.int32, (8, 128), 1)
    row = lax.broadcasted_iota(jnp.int32, (8, 128), 0)
    trainer_lane = jnp.zeros((8, 128), jnp.int32)
    for i in range(8):
        trainer_lane = jnp.where(lane % 8 == i, trainer[i], trainer_lane)
    expert = jnp.full((8, 128), -1, jnp.int32)
    gate_lane = jnp.zeros((8, 128), F32)
    for r in range(4):
        for k in range(2):
            expert = jnp.where((row == r) & (lane // 8 == k), rollout[slots[k, r]], expert)
            term = (lane >= 16 + 3 * k) & (lane < 19 + 3 * k)
            gate_lane = jnp.where((row == r) & term, gates[k, r], gate_lane)
    high = gate_lane.astype(BF).astype(F32)
    middle = (gate_lane - high).astype(BF).astype(F32)
    low = gate_lane - high - middle
    term = (lane + 2) % 3
    routing = jnp.where(expert == trainer_lane, 1.0, 0.0)
    routing = routing + jnp.where(term == 0, high, jnp.where(term == 1, middle, low))
    own_rows = x_in[...].astype(F32)
    for d in range(NZ):
        tiles = [own_rows[d * 28 : (d + 1) * 28], routing[0:4]]
        pieces[d] = jnp.concatenate(tiles, axis=0).astype(BF)
    pl.semaphore_wait(barrier, len(peers))

    sent = []

    def send(src, dst, s_sem, r_sem, peer):
        copy = pltpu.make_async_remote_copy(
            src_ref=src, dst_ref=dst, send_sem=s_sem, recv_sem=r_sem,
            device_id=peer, device_id_type=MESH,
        )
        copy.start()
        sent.append(copy)
        return copy

    piece = [
        send(pieces.at[at_z(d)], got.at[z], s_piece.at[d - 1], r_piece.at[d - 1], on_z(d))
        for d in FAR_FIRST
    ]
    loads[6].wait()
    loads[17].wait()
    turned = lax.dot_general(
        by_row[...], q_in[...], (((0,), (0,)), ((), ())), preferred_element_type=F32
    )
    q_send[...] = turned.astype(BF).reshape(4, 8, 16, 128)
    q_y = [
        send(q_send.at[:, at_y(d)], q_col.at[y], s_qy.at[d - 1], r_qy.at[d - 1], on_y(d))
        for d in FAR_FIRST
    ]
    got[z] = pieces[z]
    q_col[y] = q_send[:, y]
    loads[5].wait()
    keys[c, z] = key_own[...]

    loads[7].wait()
    for copy in piece:
        copy.wait_recv()
    turned = dot(perm[...], got[...].reshape(256, 128)).astype(BF)
    for t in range(8):
        rows[x, c, y, :, t * 128 : (t + 1) * 128] = turned[t * 32 : (t + 1) * 32]

    def block(xi, yi):
        return rows.at[xi, c, yi]

    origins, x_plus, x_minus, far = [], [], [], []

    def to_x(origin):
        k = len(origins)
        origins.append(origin)
        b = block(x, origin)
        x_plus.append(send(b, b, s_x.at[0, k], r_x.at[0, k], on_x(1)))
        x_minus.append(send(b, b, s_x.at[1, k], r_x.at[1, k], on_x(3)))

    def pass_on(k):
        x_minus[k].wait_recv()
        if k in FORWARD_MINUS:
            b = block(at_x(1), origins[k])
            far.append(send(b, b, s_fwd.at[k], r_fwd.at[k], on_x(3)))
        x_plus[k].wait_recv()
        if k in FORWARD_PLUS:
            b = block(at_x(3), origins[k])
            far.append(send(b, b, s_fwd.at[k], r_fwd.at[k], on_x(1)))

    own = block(x, y)
    y_copies = [
        send(own, own, s_ring.at[i], r_ring.at[i], on_y(sign * d))
        for i, d in enumerate((1, -1, 2, -2))
    ]
    to_x(y)
    key_z = [
        send(key_own, keys.at[c, z], s_key.at[d - 1], r_key.at[d - 1], on_z(d))
        for d in FAR_FIRST
    ]
    for copy in q_y:
        copy.wait_recv()
    q_x = [
        send(q_col.at[:, at_x(d)], q_own.at[x], s_qx.at[d - 1], r_qx.at[d - 1], on_x(d))
        for d in range(1, NX)
    ]
    q_own[x] = q_col[:, x]
    loads[8].wait()

    def line_up(i, carry):
        start = pl.multiple_of(i * 64, 64)
        w_in[pl.ds(start, 64), :] = w_raw[i].reshape(64, 896)
        return carry

    for step, d in enumerate((-1, 1, -2, 2, -3, 3, -4)):
        y_copies[step].wait_recv()
        b = block(x, at_y(sign * d))
        if d == -2:
            y_copies.append(send(b, b, s_ring.at[4], r_ring.at[4], on_y(sign)))
            far_y = send(b, b, s_ring.at[6], r_ring.at[6], on_y(2 * sign))
        if d == 2:
            y_copies.append(send(b, b, s_ring.at[5], r_ring.at[5], on_y(-sign)))
            y_copies.append(far_y)
        to_x(at_y(sign * d))
        if step == 1:
            lax.fori_loop(0, 8, line_up, 0)
        if step == 3:
            for load in loads[9:17] + loads[18:]:
                load.wait()
        if step == 5:
            for k in range(3):
                pass_on(k)
            for copy in key_z:
                copy.wait_recv()
            key_sib = send(keys.at[c], keys.at[c], s_ksib.at[0], r_ksib.at[0], sibling)

    def to_sibling(j):
        b = rows.at[at_x(X_ORDER[j]), c]
        return send(b, b, s_sib.at[j], r_sib.at[j], sibling)

    def project(group):
        for j in group:
            xi = at_x(X_ORDER[j])

            def body(ci, carry):
                routing = rows[xi, ci, :, :, 896:1024].reshape(256, 128)
                mask = dot(routing, mask_in[...])
                values = dot_nt(rows[xi, ci, :, :, 0:896].reshape(256, 896), w_in[...])
                first = (values * mask[:, :512]).astype(BF)
                second = (values * mask[:, 512:]).astype(BF)
                picked = dot(first, pick[0:512, :]) + dot(second, pick[512:1024, :])
                picked = picked.astype(BF).reshape(8, 32, 128)
                part[:, j, pl.ds(pl.multiple_of(ci * 32, 32), 32), :] = picked
                return carry

            lax.fori_loop(0, 2, body, 0)
        js = pl.ds(group[0], len(group))
        return [
            send(
                part.at[at_z(d), js], part_got.at[d - 1, js],
                s_part.at[group[0], d - 1], r_part.at[group[0], d - 1], on_z(d),
            )
            for d in FAR_FIRST
        ]

    def activate(group, arriving):
        for copy in arriving:
            copy.wait_recv()
        for j in group:
            xi = at_x(X_ORDER[j])
            total = part[z, j].astype(F32)
            for d in range(7):
                total = total + part_got[d, j].astype(F32)
            up = pltpu.roll(total, 64, 1)
            routing = rows[xi, :, z, :, 896:1024].reshape(64, 128)
            value = total / (1.0 + jnp.exp(-total)) * up * dot(routing, gate[...])
            lane = lax.broadcasted_iota(jnp.int32, (32, 128), 1)
            packed = jnp.where(lane < 64, value[0:32], pltpu.roll(value[32:64], 64, 1))
            hid[z, j] = packed.astype(BF)
        js = pl.ds(group[0], len(group))
        return [
            send(
                hid.at[z, js], hid.at[z, js],
                s_hid.at[group[0], d - 1], r_hid.at[group[0], d - 1], on_z(d),
            )
            for d in FAR_FIRST
        ]

    def project_down(group, arriving):
        for copy in arriving:
            copy.wait_recv()
        copies = []
        for j in group:
            xi = at_x(X_ORDER[j])

            def body(i, carry):
                ci = lax.rem(1 - c + i, 2)
                routing = rows[xi, ci, :, :, 896:1024].reshape(256, 128)
                wide = dot(hid[:, j].reshape(256, 128), spread[ci]) * dot(routing, mask_out[...])
                dense = (wide[:, :256] + wide[:, 256:]).astype(BF)
                share[j, ci] = dot(dense, w_out[...]).astype(BF).reshape(8, 32, 896)
                return carry

            lax.fori_loop(0, 2, body, 0)
            copies.append(
                send(share.at[j, 1 - c], share_sib.at[j], s_ssib.at[j], r_ssib.at[j], sibling)
            )
        return copies

    def own_share(j, target):
        return share[j, c, target].astype(F32) + share_sib[j, target].astype(F32)

    def move_sum(group, i, offset, to, arrived):
        js = pl.ds(group[0], len(group))
        target = at_y(sign * offset)
        for j in group:
            value = own_share(j, target)
            for k in arrived:
                value = value + ring_in[k, j].astype(F32)
            ring_out[i, j] = value.astype(BF)
        return send(
            ring_out.at[i, js], ring_in.at[i, js],
            s_red.at[group[0], i], r_red.at[group[0], i], on_y(sign * to),
        )

    def reduce_first(group, arriving):
        for copy in arriving:
            copy.wait_recv()
        hops = ((4, 3), (3, 2), (-3, -2), (2, 1), (-2, -1))
        return [move_sum(group, i, offset, to, ()) for i, (offset, to) in enumerate(hops)]

    def reduce_second(group, arriving):
        for i in (4, 2):
            arriving[i].wait_recv()
        copies = [move_sum(group, 6, -1, -1, (2, 4))]
        for i in (3, 1, 0):
            arriving[i].wait_recv()
        return copies + [move_sum(group, 5, 1, 1, (0, 1, 3))]

    def ring_step(group, step, state):
        if step == 1:
            for copy in state:
                copy.wait_recv()
        new = [None, None]
        for way, hops in ((0, 4), (1, 3)):
            if step > hops:
                new[way] = state[way]
                continue
            arrived = ()
            if step > 1:
                state[way].wait_recv()
                arrived = (way * 4 + step - 2,)
            toward = 1 - 2 * way
            new[way] = move_sum(
                group, way * 4 + step - 1, toward * (hops + 1 - step), toward, arrived
            )
        return new

    def reduce_end(group, arriving, last=(5, 6)):
        for copy in arriving:
            copy.wait_recv()
        copies = []
        for j in group:
            value = own_share(j, y)
            for k in last:
                value = value + ring_in[k, j].astype(F32)
            value = value.astype(BF)
            tiles = [value[:, t * 128 : (t + 1) * 128] for t in range(7)]
            tiles = jnp.concatenate(tiles + [jnp.zeros((32, 128), BF)], axis=0)
            back_out[j] = dot(perm_t[...], tiles).astype(BF).reshape(8, 32, 128)
            for d in FAR_FIRST + (0,):
                if j == 0 and d == 0:
                    back_got[j, z] = back_out[j, z]
                    continue
                copies.append(
                    send(
                        back_out.at[j, at_z(d)], back_got.at[j, z],
                        s_back.at[j, d], r_back.at[j, d], on_xz(X_ORDER[j], d),
                    )
                )
        return copies

    def absorb():
        for copy in q_x:
            copy.wait_recv()
        key_sib.wait_recv()
        wide = dot(q_own[...].reshape(512, 128), repeat[...])
        row = lax.broadcasted_iota(jnp.int32, (512, 512), 0)
        lane = lax.broadcasted_iota(jnp.int32, (512, 512), 1)
        head = (lane // 256) * 2 + (lane // 16) % 2
        wide = jnp.where(row % 4 == head, wide, 0.0).astype(BF)
        lat_own[...] = dot(wide, keys[...].reshape(512, 512)).astype(BF).reshape(4, 8, 16, 512)
        copies = [
            send(lat_own.at[:, at_y(d)], lat_col.at[y], s_ly.at[d - 1], r_ly.at[d - 1], on_y(d))
            for d in FAR_FIRST
        ]
        lat_col[y] = lat_own[:, y]
        return copies

    def latent_x(arriving):
        for copy in arriving:
            copy.wait_recv()
        copies = [
            send(lat_col.at[:, at_x(d)], lat_got.at[x], s_lx.at[d - 1], r_lx.at[d - 1], on_x(d))
            for d in range(1, NX)
        ]
        lat_got[x] = lat_col[:, x]
        return copies

    def latent_end(arriving):
        for copy in arriving:
            copy.wait_recv()
        turned = dot(by_row[...], lat_got[...].reshape(512, 512)).astype(BF)
        lat_rows[...] = turned.reshape(4, 128, 512)

    def attend(r):
        scores = dot_nt(lat_rows[r], cache[r])
        scores = scores + lax.dot_general(
            q_rope[r], k_rope[r], (((0,), (0,)), ((), ())), preferred_element_type=F32
        )
        scores = scores * SCORE_SCALE
        place = lax.broadcasted_iota(jnp.int32, (128, 512), 1)
        scores = jnp.where(place < lengths[r], scores, -jnp.inf)
        raised = jnp.exp(scores - jnp.max(scores, axis=1, keepdims=True))
        attention = (raised / jnp.sum(raised, axis=1, keepdims=True)).astype(BF)
        out_latent[r] = dot(attention, cache[r]).astype(BF)

    one, two, three = (0,), (1, 2), (3,)
    sib = [to_sibling(0)]
    sib[0].wait_recv()
    part_1 = project(one)
    for k in range(3, 8):
        pass_on(k)
    sib.append(to_sibling(1))
    sib.append(to_sibling(2))
    lat_y = absorb()
    hid_1 = activate(one, part_1)
    sib[1].wait_recv()
    sib[2].wait_recv()
    part_2 = project(two)
    for copy in far:
        copy.wait_recv()
    sib.append(to_sibling(3))
    sums_1 = project_down(one, hid_1)
    sib[3].wait_recv()
    part_3 = project(three)
    sums_1 = ring_step(one, 1, sums_1)
    hid_2 = activate(two, part_2)
    lat_x = latent_x(lat_y)
    sums_1 = ring_step(one, 2, sums_1)
    hid_3 = activate(three, part_3)
    sums_1 = ring_step(one, 3, sums_1)
    sums_2 = project_down(two, hid_2)
    sums_1 = ring_step(one, 4, sums_1)
    sums_3 = project_down(three, hid_3)
    sums_2 = ring_step(two, 1, sums_2)
    sums_3 = ring_step(three, 1, sums_3)
    backs = reduce_end(one, sums_1, (3, 6))
    latent_end(lat_x)
    sums_2 = ring_step(two, 2, sums_2)
    sums_3 = ring_step(three, 2, sums_3)
    attend(0)
    sums_2 = ring_step(two, 3, sums_2)
    sums_3 = ring_step(three, 3, sums_3)
    attend(1)
    sums_2 = ring_step(two, 4, sums_2)
    sums_3 = ring_step(three, 4, sums_3)
    attend(2)
    backs += reduce_end(two, sums_2, (3, 6))
    backs += reduce_end(three, sums_3, (3, 6))
    attend(3)

    for copy in backs:
        copy.wait_recv()
    for d in range(NZ):
        total = back_got[0, d].astype(F32)
        for j in range(1, NX):
            total = total + back_got[j, d].astype(F32)
        for t in range(7):
            first = (d * 7 + t) * 128
            out_rows[:, first : first + 128] = total[t * 4 : t * 4 + 4].astype(BF)
    for copy in sent:
        copy.wait_send()


def exchange(*operands):
    dma = pltpu.SemaphoreType.DMA
    sems = [
        (7,), (7,), (2, 8), (8,), (4,),
        (4, 7), (4, 7), (4,), (4, 7), (4, 8),
        (7,), (1,), (7,), (3,), (7,), (3,),
    ]
    vmem = pl.BlockSpec(memory_space=pltpu.VMEM)
    operands = list(operands) + constants()
    smem = (1, 2, 3, 4, 12)
    landing = [
        (pltpu.SMEM if i in smem else pltpu.VMEM)(a.shape, a.dtype) for i, a in enumerate(operands)
    ]
    return pl.pallas_call(
        kernel,
        out_shape=(
            jax.ShapeDtypeStruct((4, 7168), BF),
            jax.ShapeDtypeStruct((4, 128, 512), BF),
        ),
        in_specs=[pl.BlockSpec(memory_space=pltpu.HBM)] * len(operands),
        out_specs=(vmem, vmem),
        scratch_shapes=landing
        + [
            pltpu.VMEM((8, 32, 128), BF),
            pltpu.VMEM((512, 896), BF),
            pltpu.VMEM((4, 128, 512), BF),
            pltpu.VMEM((4, 8, 16, 128), BF),
            dma((len(operands),)),
            pltpu.VMEM((8, 32, 128), BF),
            pltpu.VMEM((4, 2, 8, 32, 1024), BF),
            pltpu.VMEM((8, 4, 64, 128), BF),
            pltpu.VMEM((7, 4, 64, 128), BF),
            pltpu.VMEM((8, 4, 32, 128), BF),
            pltpu.VMEM((4, 2, 8, 32, 896), BF),
            pltpu.VMEM((4, 8, 32, 896), BF),
            pltpu.VMEM((7, 4, 32, 896), BF),
            pltpu.VMEM((7, 4, 32, 896), BF),
            pltpu.VMEM((4, 8, 32, 128), BF),
            pltpu.VMEM((4, 8, 32, 128), BF),
            pltpu.VMEM((2, 8, 32, 512), BF),
            pltpu.VMEM((8, 4, 16, 128), BF),
            pltpu.VMEM((4, 8, 16, 128), BF),
            pltpu.VMEM((4, 8, 16, 512), BF),
            pltpu.VMEM((8, 4, 16, 512), BF),
            pltpu.VMEM((4, 8, 16, 512), BF),
        ]
        + [dma(shape) for shape in sems for _ in range(2)],
        compiler_params=pltpu.CompilerParams(
            collective_id=0, has_side_effects=True, vmem_limit_bytes=60 * 1024 * 1024
        ),
        cost_estimate=pl.CostEstimate(
            flops=6_000_000_000, bytes_accessed=8_000_000, transcendentals=500_000
        ),
    )(*operands)


def place(rows, latent):
    def body(rows_in, latent_in, rows_out, latent_out):
        rows_out[...] = rows_in[...]
        latent_out[...] = latent_in[...]

    vmem = pl.BlockSpec(memory_space=pltpu.VMEM)
    return pl.pallas_call(
        body,
        out_shape=tuple(jax.ShapeDtypeStruct(a.shape, a.dtype) for a in (rows, latent)),
        in_specs=[vmem, vmem],
        out_specs=(vmem, vmem),
    )(rows, latent)


def on_device(
    query_nope,
    query_rope,
    latent_cache,
    key_rope,
    lengths,
    key_weight,
    expert_input,
    route_slots,
    route_gates,
    trainer_gate_up,
    trainer_down,
    trainer_order,
    rollout_order,
):
    expert_output, latent_output = exchange(
        expert_input.reshape(4, 56, 128).transpose(1, 0, 2).reshape(224, 128),
        route_slots.T,
        route_gates.T,
        trainer_order,
        rollout_order,
        trainer_gate_up,
        trainer_down.reshape(256, 896),
        key_weight.reshape(32, 512),
        query_nope.reshape(512, 128),
        latent_cache,
        query_rope.transpose(0, 2, 1),
        key_rope.transpose(0, 2, 1),
        lengths,
    )
    expert_output, latent_output = place(expert_output, latent_output)
    return (latent_output, expert_output)


def solution(mesh):
    in_specs = (
        P(("dp", "expert"), None, None),
        P(("dp", "expert"), None, None),
        P(("dp", "expert"), None, None),
        P(("dp", "expert"), None, None),
        P(("dp", "expert")),
        P("expert", "dp", None),
        P(("dp", "expert"), None),
        P(("dp", "expert"), None),
        P(("dp", "expert"), None),
        P(None, "expert", None, "dp"),
        P(None, "expert", "dp"),
        P(),
        P(),
    )
    out_specs = (P(("dp", "expert"), None, None), P(("dp", "expert"), None))
    return jax.shard_map(
        on_device, mesh=mesh, in_specs=in_specs, out_specs=out_specs, check_vma=False
    )
```
